512 devices in a mesh: row: 32 (over x_lo, z), col: 16 (over x_hi, y, core).
Axes of the slice: x: 4 (x_hi: 2, x_lo: 2; x = x_hi * 2 + x_lo), y: 4, z: 16, core: 2. Of those that a mesh axis runs over, the one named last changes fastest.
Arguments:
- pair_state: bfloat16 [512, 512, 128], P('row', 'col'), may hold values from -6 to 6
- sequence_embedding: bfloat16 [256, 32768], P('row', 'col'), may hold values from -6 to 6
- token_valid_mask: int32 [512], replicated, may hold values 0 or 1
- sequence_present_flags: int32 [256], P('row'), may hold values 0 or 1
- triangle_input_weight: bfloat16 [128, 640], replicated, may hold values from -0.5 to 0.5
- triangle_output_weight: bfloat16 [128, 128], replicated, may hold values from -0.5 to 0.5
- pair_head_bias: bfloat16 [128, 8], replicated, may hold values from -30 to 30
- sequence_entry_matrix: bfloat16 [64, 512], replicated, may hold values from -0.75 to 0.75
- sequence_exit_matrix: bfloat16 [256, 64], replicated, may hold values from -0.375 to 0.375
Outputs:
- coupling_refreshed: bfloat16 [512, 512, 128], P('row', 'col')
- sequence_refreshed: bfloat16 [256, 32768], P('row', 'col')
The draws below stay inside these ranges and needn't reach their ends.
All inputs are finite; a program needn't handle non-finite values. No bound on the sum of `sequence_present_flags` on one device may be relied on, other than what follows from the above.
Results may differ from the reference program's by a relative error of at most 0.0073.
Values may be sent and summed in bfloat16 or wider, within the bound.
No kernel may reach another device: no remote copies, remote signals or barrier semaphores. Data moves between devices by JAX's collectives and lax.ppermute only.
A program may use at most 64 MiB of HBM per device.

```python
import math
import jax
import jax.numpy as jnp
from jax import lax

C = 128
SEQUENCE_FEATURES = 64
ATTENDER_TOTAL = 8
SINGLE_DIMENSION = 32
RESIDUE_TOTAL = 512
SEQUENCE_TOTAL = 256
PAYLOAD_FEATURES = 256


def draw_pair_head_bias(key, part):
    key = jax.random.fold_in(key, 11)
    base = jax.random.truncated_normal(jax.random.fold_in(key, 1), -4.0, 4.0, (C, ATTENDER_TOTAL), jnp.float32)
    head_log = jax.random.uniform(jax.random.fold_in(key, 2), (1, ATTENDER_TOTAL), jnp.float32, math.log(0.7), math.log(2.5))
    return (base * jnp.exp(head_log) / math.sqrt(C)).astype(jnp.bfloat16)


def with_ends(drawn, key, low, largest):
    spot = [jax.random.randint(jax.random.fold_in(key, axis), (), 0, length) for axis, length in enumerate(drawn.shape)]
    longest = drawn.shape.index(max(drawn.shape))
    next_to = spot[:longest] + [(spot[longest] + 1) % drawn.shape[longest]] + spot[longest + 1:]
    return drawn.at[tuple(spot)].set(low).at[tuple(next_to)].set(largest)


def levels(key, dims, pieces, low, largest):
    level, own = 1.0, jax.random.fold_in(key, 6)
    for position, parts in pieces:
        draws = jnp.exp(jax.random.uniform(jax.random.fold_in(own, position), (parts,), jnp.float32, low / len(pieces), largest / len(pieces)))
        level = level * jnp.repeat(draws, dims[position] // parts).reshape([-1 if axis == position else 1 for axis in range(len(dims))])
    return level


def normal_values(rng, shape, width, limit, split=(), held_as=jnp.bfloat16):
    result = jax.random.normal(rng, shape, jnp.float32) * width
    if len(split) > 0:
        result = levels(rng, shape, split, -0.22, 0.18) * result
    return jnp.clip(result, min=-limit, max=limit).astype(held_as)


def setup_inputs(seed: int = 0) -> dict:
    key_list = jax.random.split(jax.random.key(seed), 10)
    pair_state = normal_values(key_list[0], (RESIDUE_TOTAL, RESIDUE_TOTAL, C), 1.0, 6.0, ((0, 32), (1, 16)))
    sequence_embedding = normal_values(key_list[1], (SEQUENCE_TOTAL, RESIDUE_TOTAL * SEQUENCE_FEATURES), 1.0, 6.0, ((0, 32), (1, 16)))
    token_valid_mask = with_ends((jax.random.randint(key_list[2], (RESIDUE_TOTAL,), 0, 8) < 7).astype(jnp.int32), jax.random.fold_in(key_list[2], 1), 0, 1)
    sequence_present_flags = with_ends((jax.random.randint(key_list[3], (SEQUENCE_TOTAL,), 0, 4) < 3).astype(jnp.int32), jax.random.fold_in(key_list[3], 1), 0, 1)
    triangle_input_weight = normal_values(key_list[4], (C, 5 * C), C ** -0.5, 0.5)
    triangle_output_weight = normal_values(key_list[5], (C, C), C ** -0.5, 0.5)
    pair_head_bias = draw_pair_head_bias(jax.random.fold_in(key_list[9], 71), 0)
    sequence_entry_matrix = normal_values(key_list[7], (SEQUENCE_FEATURES, 2 * PAYLOAD_FEATURES), SEQUENCE_FEATURES ** -0.5, 0.75)
    sequence_exit_matrix = normal_values(key_list[8], (PAYLOAD_FEATURES, SEQUENCE_FEATURES), PAYLOAD_FEATURES ** -0.5, 0.375)
    return dict(pair_state=pair_state, sequence_embedding=sequence_embedding, token_valid_mask=token_valid_mask, sequence_present_flags=sequence_present_flags, triangle_input_weight=triangle_input_weight, triangle_output_weight=triangle_output_weight, pair_head_bias=pair_head_bias, sequence_entry_matrix=sequence_entry_matrix, sequence_exit_matrix=sequence_exit_matrix)


epsilon = 1e-05

def apply_layer_norm(array, along):
    average = lax.optimization_barrier(jnp.mean(array, axis=along, keepdims=True))
    centred = array - average
    spread = lax.optimization_barrier(jnp.mean(centred * centred, axis=along, keepdims=True))
    return centred * lax.rsqrt(spread + epsilon)

def reference(pair_state, sequence_embedding, token_valid_mask, sequence_present_flags, triangle_input_weight, triangle_output_weight, pair_head_bias, sequence_entry_matrix, sequence_exit_matrix):
    valid = token_valid_mask.astype(jnp.float32)
    pair_valid = valid[:, None] * valid[None, :]
    normed = apply_layer_norm(pair_state.astype(jnp.float32), 2).astype(jnp.bfloat16)
    projected = jnp.einsum('ijd,de->ije', normed.astype(jnp.float32), triangle_input_weight.astype(jnp.float32))
    left_proj = (jax.nn.sigmoid(projected[..., :C]) * projected[..., C:2 * C] * pair_valid[..., None]).astype(jnp.bfloat16)
    right_proj = (jax.nn.sigmoid(projected[..., 2 * C:3 * C]) * projected[..., 3 * C:4 * C] * pair_valid[..., None]).astype(jnp.bfloat16)
    out_gate = jax.nn.sigmoid(projected[..., 4 * C:])
    crossed = jnp.einsum('ikc,jkc->ijc', left_proj.astype(jnp.float32), right_proj.astype(jnp.float32))
    crossed_norm = apply_layer_norm(crossed, 2).astype(jnp.bfloat16)
    update = jnp.einsum('ijc,cd->ijd', crossed_norm.astype(jnp.float32), triangle_output_weight.astype(jnp.float32))
    coupling_refreshed = (pair_state.astype(jnp.float32) + out_gate * update).astype(jnp.bfloat16)
    normed_next = apply_layer_norm(coupling_refreshed.astype(jnp.float32), 2).astype(jnp.bfloat16)
    scores = jnp.einsum('ijc,ch->hij', normed_next.astype(jnp.float32), pair_head_bias.astype(jnp.float32))
    scores = scores + ((valid - 1.0) * 1000000000.0)[None, None, :]
    row_top = lax.optimization_barrier(jnp.max(scores, axis=2, keepdims=True))
    exponent = jnp.exp(scores - row_top)
    attention_factors = (exponent / lax.optimization_barrier(jnp.sum(exponent, axis=2, keepdims=True))).astype(jnp.bfloat16)
    sequence_slab = sequence_embedding.reshape(SEQUENCE_TOTAL, RESIDUE_TOTAL, SEQUENCE_FEATURES).astype(jnp.float32)
    alignment_normed = apply_layer_norm(sequence_slab, 2).astype(jnp.bfloat16)
    triangle_mixed = jnp.einsum('cla,ag->clg', alignment_normed.astype(jnp.float32), sequence_entry_matrix.astype(jnp.float32))
    payload_vectors = triangle_mixed[..., :PAYLOAD_FEATURES].astype(jnp.bfloat16)
    sequence_switch = jax.nn.sigmoid(triangle_mixed[..., PAYLOAD_FEATURES:])
    payload_by_attender = payload_vectors.astype(jnp.float32).reshape(SEQUENCE_TOTAL, RESIDUE_TOTAL, ATTENDER_TOTAL, SINGLE_DIMENSION)
    coupling_smoothed_sequences = jnp.einsum('rgl,zlrf->zgrf', attention_factors.astype(jnp.float32), payload_by_attender).reshape(SEQUENCE_TOTAL, RESIDUE_TOTAL, PAYLOAD_FEATURES)
    switched_product = (sequence_switch * coupling_smoothed_sequences).astype(jnp.bfloat16)
    final_output = jnp.einsum('tga,aq->tgq', switched_product.astype(jnp.float32), sequence_exit_matrix.astype(jnp.float32))
    sequence_refreshed = (sequence_slab + sequence_present_flags.astype(jnp.float32)[:, None, None] * final_output).astype(jnp.bfloat16)
    return (coupling_refreshed, sequence_refreshed.reshape(SEQUENCE_TOTAL, RESIDUE_TOTAL * SEQUENCE_FEATURES))
```

```python
import jax
import jax.numpy as jnp
from jax import lax
from jax.sharding import PartitionSpec as P

epsilon = 1e-05


def apply_layer_norm(array, along):
    average = jnp.mean(array, axis=along, keepdims=True)
    centred = array - average
    spread = jnp.mean(centred * centred, axis=along, keepdims=True)
    return centred * lax.rsqrt(spread + epsilon)


def exchange(blocks, axis):
    return lax.all_to_all(blocks, axis, split_axis=0, concat_axis=0, tiled=True)


def shards(
    pair_state,
    sequence_embedding,
    token_valid_mask,
    sequence_present_flags,
    triangle_input_weight,
    triangle_output_weight,
    pair_head_bias,
    sequence_entry_matrix,
    sequence_exit_matrix,
):
    rows_here, columns_here, channels = pair_state.shape
    heads = pair_head_bias.shape[1]
    value_width = sequence_exit_matrix.shape[0]
    features = sequence_entry_matrix.shape[0]
    msa_rows = sequence_embedding.shape[0]
    row_index = lax.axis_index("row")
    col_index = lax.axis_index("col")
    row_size = lax.axis_size("row")
    col_size = lax.axis_size("col")
    fanout = row_size // col_size
    tokens = row_size * rows_here
    patch = rows_here * columns_here
    channels_here = channels // row_size
    parts = col_size // channels_here
    part = tokens // parts

    sequence_all = lax.all_gather(sequence_embedding, "col", axis=0)

    row_valid = lax.dynamic_slice_in_dim(token_valid_mask, row_index * rows_here, rows_here).astype(
        jnp.float32
    )
    col_valid = lax.dynamic_slice_in_dim(
        token_valid_mask, col_index * columns_here, columns_here
    ).astype(jnp.float32)
    patch_valid = (col_valid[:, None] * row_valid[None, :]).reshape(1, patch)
    normed = apply_layer_norm(pair_state.astype(jnp.float32), 2).astype(jnp.bfloat16)
    normed = jnp.transpose(normed, (1, 0, 2)).reshape(patch, channels)
    projected = jnp.einsum(
        "pd,de->ep", normed, triangle_input_weight, preferred_element_type=jnp.float32
    )
    left = (
        jax.nn.sigmoid(projected[:channels]) * projected[channels : 2 * channels] * patch_valid
    ).astype(jnp.bfloat16)
    right = (
        jax.nn.sigmoid(projected[2 * channels : 3 * channels])
        * projected[3 * channels : 4 * channels]
        * patch_valid
    ).astype(jnp.bfloat16)
    out_gate = jax.nn.sigmoid(projected[4 * channels :])

    sent = jnp.stack(
        [left.reshape(row_size, channels_here, patch), right.reshape(row_size, channels_here, patch)],
        axis=1,
    ).reshape(row_size, 2 * channels_here, patch)
    got = exchange(sent, "row").reshape(
        row_size, 2, channels_here, columns_here, rows_here
    )
    got = jnp.transpose(got, (1, 2, 3, 0, 4)).reshape(2, channels_here, columns_here, tokens)
    left_parts = jnp.transpose(
        got[0].reshape(channels_here, columns_here, parts, part), (0, 2, 1, 3)
    )
    right_parts = jnp.broadcast_to(
        got[1][:, None], (channels_here, parts, columns_here, tokens)
    )
    sent = jnp.concatenate([left_parts, right_parts], axis=3).reshape(
        col_size, columns_here, part + tokens
    )
    got = exchange(sent, "col").reshape(tokens, part + tokens)
    crossed = jnp.einsum(
        "kj,ki->ji", got[:, part:], got[:, :part], preferred_element_type=jnp.float32
    ).astype(jnp.bfloat16)
    got = exchange(crossed.reshape(col_size, columns_here, part), "col").reshape(
        channels_here, parts, columns_here, row_size // parts, rows_here
    )
    sent = jnp.transpose(got, (1, 3, 0, 2, 4)).reshape(row_size, channels_here, patch)
    crossed = exchange(sent, "row").reshape(channels, patch).astype(jnp.float32)

    crossed_norm = apply_layer_norm(crossed, 0).astype(jnp.bfloat16)
    update = jnp.einsum(
        "cp,cd->dp", crossed_norm, triangle_output_weight, preferred_element_type=jnp.float32
    )
    update = (out_gate * update).reshape(channels, columns_here, rows_here)
    coupling_refreshed = (
        pair_state.astype(jnp.float32) + jnp.transpose(update, (2, 1, 0))
    ).astype(jnp.bfloat16)
    normed_next = apply_layer_norm(coupling_refreshed.astype(jnp.float32), 2).astype(jnp.bfloat16)
    scores = jnp.einsum(
        "ijc,ch->jih", normed_next, pair_head_bias, preferred_element_type=jnp.float32
    ).reshape(columns_here, rows_here * heads)
    scores = scores + ((col_valid - 1.0) * 1000000000.0)[:, None]

    moves = []
    for row in range(row_size):
        for col in range(col_size):
            target = ((row % fanout) * col_size + col) * col_size + row // fanout
            moves.append((row * col_size + col, target))
    scores = lax.ppermute(scores, ("row", "col"), moves)
    scores = exchange(
        jnp.broadcast_to(scores[None], (row_size,) + scores.shape), "row"
    ).reshape(fanout, tokens, rows_here * heads)
    exponent = jnp.exp(scores - jnp.max(scores, axis=1, keepdims=True))
    weights = (exponent / jnp.sum(exponent, axis=1, keepdims=True)).astype(jnp.bfloat16)

    sequence_all = sequence_all.reshape(col_size, msa_rows, columns_here, features)
    sequence_all = apply_layer_norm(sequence_all.astype(jnp.float32), 3).astype(jnp.bfloat16)
    values = jnp.einsum(
        "qsjf,fg->sqjg",
        sequence_all,
        sequence_entry_matrix[:, :value_width],
        preferred_element_type=jnp.float32,
    ).astype(jnp.bfloat16).reshape(msa_rows, tokens, value_width)
    sequence_slab = sequence_embedding.reshape(msa_rows, columns_here, features).astype(jnp.float32)
    sequence_normed = apply_layer_norm(sequence_slab, 2).astype(jnp.bfloat16)
    sequence_switch = jax.nn.sigmoid(
        jnp.einsum(
            "sjf,fg->sjg",
            sequence_normed,
            sequence_entry_matrix[:, value_width:],
            preferred_element_type=jnp.float32,
        )
    )
    averaged = jnp.einsum(
        "mjp,sjg->smpg", weights, values, preferred_element_type=jnp.float32
    ).reshape(msa_rows, fanout * rows_here, heads, value_width)
    own = (
        lax.broadcasted_iota(jnp.int32, (heads, value_width), 1) // (value_width // heads)
        == lax.broadcasted_iota(jnp.int32, (heads, value_width), 0)
    )
    averaged = jnp.sum(jnp.where(own[None, None], averaged, 0.0), axis=2)
    switched = (sequence_switch * averaged).astype(jnp.bfloat16)
    final_output = jnp.einsum(
        "sig,gf->sif", switched, sequence_exit_matrix, preferred_element_type=jnp.float32
    )
    sequence_refreshed = (
        sequence_slab + sequence_present_flags.astype(jnp.float32)[:, None, None] * final_output
    ).astype(jnp.bfloat16)
    return (
        coupling_refreshed,
        sequence_refreshed.reshape(msa_rows, columns_here * features),
    )


def solution(mesh):
    placed = (P("row", "col", None), P("row", "col"), P(), P("row"), P(), P(), P(), P(), P())
    return jax.shard_map(
        shards,
        mesh=mesh,
        in_specs=placed,
        out_specs=(P("row", "col", None), P("row", "col")),
        check_vma=False,
    )
```

```python
import functools

import jax
import jax.numpy as jnp
from jax import lax
from jax.experimental import pallas as pl
from jax.experimental.pallas import tpu as pltpu
from jax.sharding import PartitionSpec as P

epsilon = 1e-05
mask_offset = 1000000000.0
score_floor = -8192.0


def apply_layer_norm(array, along):
    average = jnp.mean(array, axis=along, keepdims=True)
    centred = array - average
    spread = jnp.mean(centred * centred, axis=along, keepdims=True)
    return centred * lax.rsqrt(spread + epsilon)


def exchange(blocks, axis):
    return lax.all_to_all(blocks, axis, split_axis=0, concat_axis=0, tiled=True)


def normed_rows(array):
    average = jnp.mean(array, axis=-1, keepdims=True)
    centred = array - average
    spread = jnp.mean(centred * centred, axis=-1, keepdims=True)
    return centred * lax.rsqrt(spread + epsilon)


def project_kernel(
    row_size, col_size, mask, pair, weight, sent, gate, wide, mixed
):
    rows, columns, channels = pair.shape
    patch = rows * columns
    here = channels // row_size
    wide[...] = normed_rows(pair[...].astype(jnp.float32).reshape(patch, channels))
    normed = jnp.concatenate(
        [wide[pl.ds(k, rows, stride=columns), :] for k in range(columns)], axis=0
    ).astype(jnp.bfloat16)
    projected = lax.dot_general(
        weight[...], normed, (((0,), (1,)), ((), ())), preferred_element_type=jnp.float32
    )
    lane = lax.broadcasted_iota(jnp.int32, (1, patch), 1)
    first_row = lax.axis_index("row") * rows
    first_column = lax.axis_index("col") * columns
    row_valid = jnp.zeros((1, patch), jnp.int32)
    column_valid = jnp.zeros((1, patch), jnp.int32)
    for i in range(rows):
        row_valid = jnp.where(lane % rows == i, mask[first_row + i], row_valid)
    for k in range(columns):
        column_valid = jnp.where(lane // rows == k, mask[first_column + k], column_valid)
    valid = (row_valid * column_valid).astype(jnp.float32)
    left = jax.nn.sigmoid(projected[:channels]) * projected[channels : 2 * channels] * valid
    right = (
        jax.nn.sigmoid(projected[2 * channels : 3 * channels])
        * projected[3 * channels : 4 * channels]
        * valid
    )
    gate[...] = jax.nn.sigmoid(projected[4 * channels :])
    for r in range(row_size):
        mixed[2 * r * here : (2 * r + 1) * here, :] = left[r * here : (r + 1) * here]
        mixed[(2 * r + 1) * here : (2 * r + 2) * here, :] = right[r * here : (r + 1) * here]
    sent[...] = mixed[...].astype(jnp.bfloat16)


def update_kernel(mask, all_valid, crossed, gate, pair, weight, bias, coupling, spread, wide):
    rows, columns, channels = pair.shape
    patch = rows * columns
    lanes = bias.shape[1]
    heads = lanes // rows
    cross = crossed[...].astype(jnp.float32)
    average = jnp.mean(cross, axis=0, keepdims=True)
    centred = cross - average
    variance = jnp.mean(centred * centred, axis=0, keepdims=True)
    cross = (centred * lax.rsqrt(variance + epsilon)).astype(jnp.bfloat16)
    update = lax.dot_general(
        weight[...], cross, (((0,), (0,)), ((), ())), preferred_element_type=jnp.float32
    )
    wide[...] = (gate[...] * update).T
    lane = lax.broadcasted_iota(jnp.int32, (channels, lanes), 1)
    scores = jnp.zeros((columns, lanes), jnp.float32)
    for i in range(rows):
        line = pair[i].astype(jnp.float32) + wide[pl.ds(i, columns, stride=rows), :]
        line = line.astype(jnp.bfloat16)
        coupling[i] = line
        normed = normed_rows(line.astype(jnp.float32)).astype(jnp.bfloat16)
        own = jnp.where(lane // heads == i, bias[...], jnp.zeros((), jnp.bfloat16))
        scores = scores + jnp.dot(normed, own, preferred_element_type=jnp.float32)
    place = lax.broadcasted_iota(jnp.int32, (columns, lanes), 0)
    first_column = lax.axis_index("col") * columns
    valid = jnp.zeros((columns, lanes), jnp.int32)
    for j in range(columns):
        valid = jnp.where(place == j, mask[first_column + j], valid)
    any_valid = jnp.max(all_valid[...], axis=1, keepdims=True)
    any_valid = jnp.max(any_valid, axis=0, keepdims=True) > 0
    scores = scores + (valid.astype(jnp.float32) - 1.0) * mask_offset
    scores = jnp.where(any_valid, jnp.maximum(scores, score_floor), scores + mask_offset)
    top = jnp.max(scores, axis=0, keepdims=True).astype(jnp.bfloat16).astype(jnp.float32)
    spread[:columns, :] = jnp.exp(scores - top)
    spread[columns:, :] = jnp.broadcast_to(top, (spread.shape[0] - columns, lanes))


def shards(
    pair_state,
    sequence_embedding,
    token_valid_mask,
    sequence_present_flags,
    triangle_input_weight,
    triangle_output_weight,
    pair_head_bias,
    sequence_entry_matrix,
    sequence_exit_matrix,
):
    rows_here, columns_here, channels = pair_state.shape
    heads = pair_head_bias.shape[1]
    value_width = sequence_exit_matrix.shape[0]
    features = sequence_entry_matrix.shape[0]
    msa_rows = sequence_embedding.shape[0]
    row_index = lax.axis_index("row")
    col_index = lax.axis_index("col")
    row_size = lax.axis_size("row")
    col_size = lax.axis_size("col")
    fanout = row_size // col_size
    tokens = row_size * rows_here
    patch = rows_here * columns_here
    channels_here = channels // row_size
    left_parts = col_size // channels_here // fanout
    left_width = tokens // left_parts
    right_width = tokens // fanout
    moves = []
    for row in range(row_size):
        for col in range(col_size):
            target = ((row % fanout) * col_size + col) * col_size + row // fanout
            moves.append((row * col_size + col, target))

    vmem = pl.BlockSpec(memory_space=pltpu.VMEM)
    smem = pl.BlockSpec(memory_space=pltpu.SMEM)
    sent, out_gate = pl.pallas_call(
        functools.partial(project_kernel, row_size, col_size),
        out_shape=(
            jax.ShapeDtypeStruct((2 * channels, patch), jnp.bfloat16),
            jax.ShapeDtypeStruct((channels, patch), jnp.float32),
        ),
        in_specs=[smem, vmem, vmem],
        out_specs=(vmem, vmem),
        scratch_shapes=[
            pltpu.VMEM((patch, channels), jnp.float32),
            pltpu.VMEM((2 * channels, patch), jnp.float32),
        ],
        compiler_params=pltpu.CompilerParams(vmem_limit_bytes=32 * 1024 * 1024),
        cost_estimate=pl.CostEstimate(
            flops=10 * patch * channels * channels, bytes_accessed=2**20, transcendentals=0
        ),
    )(token_valid_mask, pair_state, triangle_input_weight)

    rider, sent = lax.optimization_barrier((sequence_embedding, sent))
    got = exchange(sent.reshape(row_size, 2 * channels_here, patch), "row")
    sequence_all = exchange(
        jnp.broadcast_to(rider[None], (col_size,) + rider.shape), "col"
    ).reshape(col_size, msa_rows, columns_here, features)
    got = got.reshape(row_size, 2, channels_here, columns_here, rows_here)
    got = jnp.transpose(got, (1, 2, 3, 0, 4))
    left = jnp.transpose(
        got[0].reshape(channels_here, columns_here, left_parts, left_width), (0, 2, 1, 3)
    ).reshape(channels_here, left_parts, 1, columns_here, left_width)
    right = jnp.transpose(
        got[1].reshape(channels_here, columns_here, col_size, fanout, rows_here), (0, 3, 1, 2, 4)
    ).reshape(channels_here, 1, fanout, columns_here, right_width)
    lead = (channels_here, left_parts, fanout, columns_here)
    sent = jnp.concatenate(
        [jnp.broadcast_to(left, lead + (left_width,)), jnp.broadcast_to(right, lead + (right_width,))],
        axis=4,
    ).reshape(col_size, columns_here, left_width + right_width)
    got = exchange(sent, "col").reshape(tokens, left_width + right_width)
    crossed = jnp.einsum(
        "kj,ki->ji",
        got[:, left_width:],
        got[:, :left_width],
        preferred_element_type=jnp.float32,
    ).astype(jnp.bfloat16)
    got = exchange(crossed.reshape(col_size, rows_here, left_width), "col").reshape(
        channels_here, left_parts, fanout, rows_here, row_size // left_parts, rows_here
    )
    sent = jnp.transpose(got, (1, 4, 0, 2, 3, 5)).reshape(row_size, channels_here, patch)
    crossed = exchange(sent, "row").reshape(channels, patch)
    coupling_refreshed, sent = pl.pallas_call(
        update_kernel,
        out_shape=(
            jax.ShapeDtypeStruct(pair_state.shape, jnp.bfloat16),
            jax.ShapeDtypeStruct((columns_here + 8, rows_here * heads), jnp.float32),
        ),
        in_specs=[smem] + [vmem] * 6,
        out_specs=(vmem, vmem),
        scratch_shapes=[pltpu.VMEM((patch, channels), jnp.float32)],
        compiler_params=pltpu.CompilerParams(vmem_limit_bytes=32 * 1024 * 1024),
        cost_estimate=pl.CostEstimate(
            flops=4 * patch * channels * channels, bytes_accessed=2**20, transcendentals=0
        ),
    )(
        token_valid_mask,
        token_valid_mask.reshape(4, -1),
        crossed,
        out_gate,
        pair_state,
        triangle_output_weight,
        jnp.tile(pair_head_bias, (1, rows_here)),
    )
    sent = sent.astype(jnp.bfloat16)

    sent = lax.ppermute(sent, ("row", "col"), moves)
    groups = [[m * col_size + b for b in range(col_size)] for m in range(fanout)]
    mine = lax.all_to_all(
        jnp.broadcast_to(sent[None], (col_size,) + sent.shape),
        "row",
        split_axis=0,
        concat_axis=0,
        axis_index_groups=groups,
        tiled=True,
    )
    swap = [(a, (a + col_size) % row_size) for a in range(row_size)]
    other = lax.ppermute(mine, "row", swap)

    sequence_all = apply_layer_norm(sequence_all.astype(jnp.float32), 3).astype(jnp.bfloat16)
    values = jnp.einsum(
        "qsjf,fg->qjsg",
        sequence_all,
        sequence_entry_matrix[:, :value_width],
        preferred_element_type=jnp.float32,
    ).astype(jnp.bfloat16).reshape(tokens, msa_rows * value_width)
    own = (
        lax.broadcasted_iota(jnp.int32, (heads, 1, value_width), 2) // (value_width // heads)
        == lax.broadcasted_iota(jnp.int32, (heads, 1, value_width), 0)
    )

    def average(got):
        got = got.astype(jnp.float32)
        tops = got[:, columns_here : columns_here + 1]
        exponent = got[:, :columns_here] * jnp.exp(tops - jnp.max(tops, axis=0, keepdims=True))
        weights = (exponent / jnp.sum(exponent, axis=(0, 1), keepdims=True)).astype(jnp.bfloat16)
        averaged = jnp.einsum(
            "jp,jx->px",
            weights.reshape(tokens, rows_here * heads),
            values,
            preferred_element_type=jnp.float32,
        ).reshape(rows_here, heads, msa_rows, value_width)
        return jnp.sum(jnp.where(own[None], averaged, 0.0), axis=1)

    mine = average(mine)
    other = average(other)
    low = row_index < col_size
    averaged = jnp.concatenate(
        [jnp.where(low, mine, other), jnp.where(low, other, mine)], axis=0
    )
    sequence_slab = sequence_embedding.reshape(msa_rows, columns_here, features).astype(jnp.float32)
    sequence_normed = apply_layer_norm(sequence_slab, 2).astype(jnp.bfloat16)
    sequence_switch = jax.nn.sigmoid(
        jnp.einsum(
            "sjf,fg->jsg",
            sequence_normed,
            sequence_entry_matrix[:, value_width:],
            preferred_element_type=jnp.float32,
        )
    )
    switched = (sequence_switch * averaged).astype(jnp.bfloat16)
    final_output = jnp.einsum(
        "isg,gf->sif", switched, sequence_exit_matrix, preferred_element_type=jnp.float32
    )
    sequence_refreshed = (
        sequence_slab + sequence_present_flags.astype(jnp.float32)[:, None, None] * final_output
    ).astype(jnp.bfloat16)
    return (
        coupling_refreshed,
        sequence_refreshed.reshape(msa_rows, columns_here * features),
    )


def solution(mesh):
    placed = (P("row", "col", None), P("row", "col"), P(), P("row"), P(), P(), P(), P(), P())
    return jax.shard_map(
        shards,
        mesh=mesh,
        in_specs=placed,
        out_specs=(P("row", "col", None), P("row", "col")),
        check_vma=False,
    )
```

```python
import functools

import jax
import jax.numpy as jnp
from jax import lax
from jax.experimental import pallas as pl
from jax.experimental.pallas import tpu as pltpu
from jax.sharding import PartitionSpec as P

epsilon = 1e-05
mask_offset = 1000000000.0
score_floor = -8192.0


def apply_layer_norm(array, along):
    average = jnp.mean(array, axis=along, keepdims=True)
    centred = array - average
    spread = jnp.mean(centred * centred, axis=along, keepdims=True)
    return centred * lax.rsqrt(spread + epsilon)


def exchange(blocks, axis):
    return lax.all_to_all(blocks, axis, split_axis=0, concat_axis=0, tiled=True)


def normed_rows(array):
    average = jnp.mean(array, axis=-1, keepdims=True)
    centred = array - average
    spread = jnp.mean(centred * centred, axis=-1, keepdims=True)
    return centred * lax.rsqrt(spread + epsilon)


def project_kernel(
    row_size, mask, pair, weight, sent, wide, mixed
):
    rows, columns, channels = pair.shape
    patch = rows * columns
    here = channels // row_size
    wide[...] = normed_rows(pair[...].astype(jnp.float32).reshape(patch, channels))
    normed = jnp.concatenate(
        [wide[pl.ds(k, rows, stride=columns), :] for k in range(columns)], axis=0
    ).astype(jnp.bfloat16)
    projected = lax.dot_general(
        weight[:, : 4 * channels], normed, (((0,), (1,)), ((), ())), preferred_element_type=jnp.float32
    )
    lane = lax.broadcasted_iota(jnp.int32, (1, patch), 1)
    first_row = lax.axis_index("row") * rows
    first_column = lax.axis_index("col") * columns
    row_valid = jnp.zeros((1, patch), jnp.int32)
    column_valid = jnp.zeros((1, patch), jnp.int32)
    for i in range(rows):
        row_valid = jnp.where(lane % rows == i, mask[first_row + i], row_valid)
    for k in range(columns):
        column_valid = jnp.where(lane // rows == k, mask[first_column + k], column_valid)
    valid = (row_valid * column_valid).astype(jnp.float32)
    left = jax.nn.sigmoid(projected[:channels]) * projected[channels : 2 * channels] * valid
    right = (
        jax.nn.sigmoid(projected[2 * channels : 3 * channels])
        * projected[3 * channels : 4 * channels]
        * valid
    )
    for r in range(row_size):
        mixed[2 * r * here : (2 * r + 1) * here, :] = left[r * here : (r + 1) * here]
        mixed[(2 * r + 1) * here : (2 * r + 2) * here, :] = right[r * here : (r + 1) * here]
    sent[...] = mixed[...].astype(jnp.bfloat16)


def update_kernel(columns, mask, all_valid, crossed, pair, gate_weight, weight, bias, coupling, spread):
    patch, channels = pair.shape
    rows = patch // columns
    lanes = bias.shape[1]
    heads = lanes // rows
    cross = crossed[...].astype(jnp.float32)
    average = jnp.mean(cross, axis=0, keepdims=True)
    centred = cross - average
    variance = jnp.mean(centred * centred, axis=0, keepdims=True)
    cross = (centred * lax.rsqrt(variance + epsilon)).astype(jnp.bfloat16)
    update = lax.dot_general(
        cross, weight[...], (((0,), (0,)), ((), ())), preferred_element_type=jnp.float32
    )
    before = pair[...].astype(jnp.float32)
    gate = jnp.dot(
        normed_rows(before).astype(jnp.bfloat16),
        gate_weight[:, 4 * channels :],
        preferred_element_type=jnp.float32,
    )
    after = (before + jax.nn.sigmoid(gate) * update).astype(jnp.bfloat16)
    coupling[...] = after
    normed = normed_rows(after.astype(jnp.float32)).astype(jnp.bfloat16)
    lane = lax.broadcasted_iota(jnp.int32, (channels, lanes), 1)
    scores = jnp.zeros((columns, lanes), jnp.float32)
    for i in range(rows):
        own = jnp.where(lane // heads == i, bias[...], jnp.zeros((), jnp.bfloat16))
        scores = scores + jnp.dot(
            normed[i * columns : (i + 1) * columns], own, preferred_element_type=jnp.float32
        )
    place = lax.broadcasted_iota(jnp.int32, (columns, lanes), 0)
    row_index = lax.axis_index("row")
    col_size = lax.axis_size("col")
    turned = (row_index + 2 * (col_size - lax.axis_index("col"))) % col_size
    first_column = (turned // 2 * 2 + row_index // col_size) * columns
    valid = jnp.zeros((columns, lanes), jnp.int32)
    for j in range(columns):
        valid = jnp.where(place == j, mask[first_column + j], valid)
    any_valid = jnp.max(all_valid[...], axis=1, keepdims=True)
    any_valid = jnp.max(any_valid, axis=0, keepdims=True) > 0
    scores = scores + (valid.astype(jnp.float32) - 1.0) * mask_offset
    scores = jnp.where(any_valid, jnp.maximum(scores, score_floor), scores + mask_offset)
    top = jnp.max(scores, axis=0, keepdims=True).astype(jnp.bfloat16).astype(jnp.float32)
    spread[:columns, :] = jnp.exp(scores - top)
    spread[columns:, :] = jnp.broadcast_to(top, (spread.shape[0] - columns, lanes))


def tile_place(row, col, col_size):
    return (col % 2) * col_size + (row + col // 2 * 2) % col_size, row // 2


def shards(
    pair_state,
    sequence_embedding,
    token_valid_mask,
    sequence_present_flags,
    triangle_input_weight,
    triangle_output_weight,
    pair_head_bias,
    sequence_entry_matrix,
    sequence_exit_matrix,
):
    rows_here, columns_here, channels = pair_state.shape
    heads = pair_head_bias.shape[1]
    value_width = sequence_exit_matrix.shape[0]
    features = sequence_entry_matrix.shape[0]
    msa_rows = sequence_embedding.shape[0]
    row_index = lax.axis_index("row")
    col_index = lax.axis_index("col")
    row_size = lax.axis_size("row")
    col_size = lax.axis_size("col")
    fanout = row_size // col_size
    tokens = row_size * rows_here
    patch = rows_here * columns_here
    channels_here = channels // row_size
    right_parts = col_size // channels_here // fanout
    left_width = tokens // fanout
    right_width = tokens // right_parts
    moves = []
    for row in range(row_size):
        for col in range(col_size):
            to_row, to_col = tile_place(row, col, col_size)
            moves.append((row * col_size + col, to_row * col_size + to_col))
    moves_back = [(b, a) for a, b in moves]

    vmem = pl.BlockSpec(memory_space=pltpu.VMEM)
    smem = pl.BlockSpec(memory_space=pltpu.SMEM)
    sent = pl.pallas_call(
        functools.partial(project_kernel, row_size),
        out_shape=jax.ShapeDtypeStruct((2 * channels, patch), jnp.bfloat16),
        in_specs=[smem, vmem, vmem],
        out_specs=vmem,
        scratch_shapes=[
            pltpu.VMEM((patch, channels), jnp.float32),
            pltpu.VMEM((2 * channels, patch), jnp.float32),
        ],
        compiler_params=pltpu.CompilerParams(vmem_limit_bytes=32 * 1024 * 1024),
        cost_estimate=pl.CostEstimate(
            flops=10 * patch * channels * channels, bytes_accessed=2**20, transcendentals=0
        ),
    )(token_valid_mask, pair_state, triangle_input_weight)

    got = exchange(sent.reshape(row_size, 2 * channels_here, patch), "row")
    pair_later, got = lax.optimization_barrier((pair_state, got))
    pair_moved = lax.ppermute(pair_later.reshape(patch, channels), ("row", "col"), moves)
    got = got.reshape(row_size, 2, channels_here, columns_here, rows_here)
    got = jnp.transpose(got, (1, 2, 3, 0, 4))
    left = jnp.transpose(
        got[0].reshape(channels_here, columns_here, col_size, fanout, rows_here), (0, 3, 1, 2, 4)
    ).reshape(channels_here, fanout, 1, columns_here, left_width)
    right = jnp.transpose(
        got[1].reshape(channels_here, columns_here, right_parts, right_width), (0, 2, 1, 3)
    ).reshape(channels_here, 1, right_parts, columns_here, right_width)
    lead = (channels_here, fanout, right_parts, columns_here)
    sent = jnp.concatenate(
        [jnp.broadcast_to(left, lead + (left_width,)), jnp.broadcast_to(right, lead + (right_width,))],
        axis=4,
    ).reshape(col_size, columns_here, left_width + right_width)
    rider = jnp.tile(
        sequence_embedding.reshape(2, -1, left_width + right_width), (col_size // 2, 1, 1)
    )
    got = exchange(jnp.concatenate([sent, rider], axis=1), "col")
    got, pair_moved = lax.optimization_barrier((got, pair_moved))
    half = got[:, columns_here:]
    half_other = lax.ppermute(half, "col", [(a, a ^ 1) for a in range(col_size)])
    first = col_index % 2 == 0
    sequence_all = jnp.concatenate(
        [jnp.where(first, half, half_other), jnp.where(first, half_other, half)], axis=1
    ).reshape(col_size // 2, 2, msa_rows, columns_here, features)
    sequence_all = jnp.roll(sequence_all, col_index, axis=0).reshape(
        col_size, msa_rows, columns_here, features
    )
    sequence_all = apply_layer_norm(sequence_all.astype(jnp.float32), 3).astype(jnp.bfloat16)
    values = jnp.einsum(
        "qsjf,fg->qjsg",
        sequence_all,
        sequence_entry_matrix[:, :value_width],
        preferred_element_type=jnp.float32,
    ).astype(jnp.bfloat16).reshape(tokens, msa_rows * value_width)
    got = got[:, :columns_here].reshape(tokens, left_width + right_width)
    crossed = jnp.einsum(
        "ki,kj->ij",
        got[:, :left_width],
        got[:, left_width:],
        preferred_element_type=jnp.float32,
    ).astype(jnp.bfloat16)
    got = exchange(crossed.reshape(col_size, rows_here, right_width), "col").reshape(
        channels_here, fanout, right_parts, rows_here, col_size // right_parts // 2, 2, columns_here
    )
    sent = jnp.transpose(got, (5, 2, 4, 1, 0, 3, 6)).reshape(
        2, col_size // 2, fanout, channels_here, patch
    )
    sent = jnp.roll(sent, col_index, axis=1).reshape(row_size, channels_here, patch)
    crossed = exchange(sent, "row").reshape(channels, patch)
    crossed, values = lax.optimization_barrier((crossed, values))
    coupling_moved, sent = pl.pallas_call(
        functools.partial(update_kernel, columns_here),
        out_shape=(
            jax.ShapeDtypeStruct((patch, channels), jnp.bfloat16),
            jax.ShapeDtypeStruct((columns_here + 8, rows_here * heads), jnp.float32),
        ),
        in_specs=[smem] + [vmem] * 6,
        out_specs=(vmem, vmem),
        compiler_params=pltpu.CompilerParams(vmem_limit_bytes=32 * 1024 * 1024),
        cost_estimate=pl.CostEstimate(
            flops=6 * patch * channels * channels, bytes_accessed=2**20, transcendentals=0
        ),
    )(
        token_valid_mask,
        token_valid_mask.reshape(4, -1),
        crossed,
        pair_moved,
        triangle_input_weight,
        triangle_output_weight,
        jnp.tile(pair_head_bias, (1, rows_here)),
    )
    coupling_refreshed = lax.ppermute(coupling_moved, ("row", "col"), moves_back).reshape(
        rows_here, columns_here, channels
    )
    sent = sent.astype(jnp.bfloat16)
    got = exchange(jnp.broadcast_to(sent[None], (row_size,) + sent.shape), "row")
    got = jnp.transpose(
        got.reshape(2, col_size // 2, fanout, columns_here + 8, rows_here * heads), (2, 1, 0, 3, 4)
    ).reshape(fanout, col_size, columns_here + 8, rows_here * heads)

    own = (
        lax.broadcasted_iota(jnp.int32, (heads, 1, value_width), 2) // (value_width // heads)
        == lax.broadcasted_iota(jnp.int32, (heads, 1, value_width), 0)
    )

    def average(got):
        got = got.astype(jnp.float32)
        tops = got[:, columns_here : columns_here + 1]
        exponent = got[:, :columns_here] * jnp.exp(tops - jnp.max(tops, axis=0, keepdims=True))
        weights = (exponent / jnp.sum(exponent, axis=(0, 1), keepdims=True)).astype(jnp.bfloat16)
        averaged = jnp.einsum(
            "jp,jx->px",
            weights.reshape(tokens, rows_here * heads),
            values,
            preferred_element_type=jnp.float32,
        ).reshape(rows_here, heads, msa_rows, value_width)
        return jnp.sum(jnp.where(own[None], averaged, 0.0), axis=1)

    averaged = jnp.concatenate([average(got[m]) for m in range(fanout)], axis=0)
    sequence_slab = sequence_embedding.reshape(msa_rows, columns_here, features).astype(jnp.float32)
    sequence_normed = apply_layer_norm(sequence_slab, 2).astype(jnp.bfloat16)
    sequence_switch = jax.nn.sigmoid(
        jnp.einsum(
            "sjf,fg->jsg",
            sequence_normed,
            sequence_entry_matrix[:, value_width:],
            preferred_element_type=jnp.float32,
        )
    )
    switched = (sequence_switch * averaged).astype(jnp.bfloat16)
    final_output = jnp.einsum(
        "isg,gf->sif", switched, sequence_exit_matrix, preferred_element_type=jnp.float32
    )
    sequence_refreshed = (
        sequence_slab + sequence_present_flags.astype(jnp.float32)[:, None, None] * final_output
    ).astype(jnp.bfloat16)
    return (
        coupling_refreshed,
        sequence_refreshed.reshape(msa_rows, columns_here * features),
    )


def solution(mesh):
    placed = (P("row", "col", None), P("row", "col"), P(), P("row"), P(), P(), P(), P(), P())
    return jax.shard_map(
        shards,
        mesh=mesh,
        in_specs=placed,
        out_specs=(P("row", "col", None), P("row", "col")),
        check_vma=False,
    )
```

```python
import functools

import jax
import jax.numpy as jnp
from jax import lax
from jax.experimental import pallas as pl
from jax.experimental.pallas import tpu as pltpu
from jax.sharding import PartitionSpec as P

epsilon = 1e-05
mask_offset = 1000000000.0
score_floor = -8192.0


def apply_layer_norm(array, along):
    average = jnp.mean(array, axis=along, keepdims=True)
    centred = array - average
    spread = jnp.mean(centred * centred, axis=along, keepdims=True)
    return centred * lax.rsqrt(spread + epsilon)


def exchange(blocks, axis):
    return lax.all_to_all(blocks, axis, split_axis=0, concat_axis=0, tiled=True)


def normed_rows(array):
    average = jnp.mean(array, axis=-1, keepdims=True)
    centred = array - average
    spread = jnp.mean(centred * centred, axis=-1, keepdims=True)
    return centred * lax.rsqrt(spread + epsilon)


def project_kernel(
    row_size, mask_far, pair_far, weight_far, sent, gate, mask, pair, weight, wide, mixed, arrived
):
    copies = [
        pltpu.make_async_copy(pair_far, pair, arrived.at[0]),
        pltpu.make_async_copy(weight_far, weight, arrived.at[1]),
        pltpu.make_async_copy(mask_far, mask, arrived.at[2]),
    ]
    for copy in copies:
        copy.start()
    for copy in copies:
        copy.wait()
    rows, columns, channels = pair.shape
    patch = rows * columns
    here = channels // row_size
    wide[...] = normed_rows(pair[...].astype(jnp.float32).reshape(patch, channels))
    normed = jnp.concatenate(
        [wide[pl.ds(k, rows, stride=columns), :] for k in range(columns)], axis=0
    ).astype(jnp.bfloat16)
    projected = lax.dot_general(
        weight[...], normed, (((0,), (1,)), ((), ())), preferred_element_type=jnp.float32
    )
    lane = lax.broadcasted_iota(jnp.int32, (1, patch), 1)
    first_row = lax.axis_index("row") * rows
    first_column = lax.axis_index("col") * columns
    row_valid = jnp.zeros((1, patch), jnp.int32)
    column_valid = jnp.zeros((1, patch), jnp.int32)
    for i in range(rows):
        row_valid = jnp.where(lane % rows == i, mask[first_row + i], row_valid)
    for k in range(columns):
        column_valid = jnp.where(lane // rows == k, mask[first_column + k], column_valid)
    valid = (row_valid * column_valid).astype(jnp.float32)
    left = jax.nn.sigmoid(projected[:channels]) * projected[channels : 2 * channels] * valid
    right = (
        jax.nn.sigmoid(projected[2 * channels : 3 * channels])
        * projected[3 * channels : 4 * channels]
        * valid
    )
    gate[...] = jax.nn.sigmoid(projected[4 * channels :])
    for r in range(row_size):
        mixed[2 * r * here : (2 * r + 1) * here, :] = left[r * here : (r + 1) * here]
        mixed[(2 * r + 1) * here : (2 * r + 2) * here, :] = right[r * here : (r + 1) * here]
    sent[...] = mixed[...].astype(jnp.bfloat16)


def update_kernel(mask, all_valid, crossed, gate, pair, weight, bias, coupling, spread, wide):
    rows, columns, channels = pair.shape
    patch = rows * columns
    lanes = bias.shape[1]
    heads = lanes // rows
    cross = crossed[...].astype(jnp.float32)
    average = jnp.mean(cross, axis=0, keepdims=True)
    centred = cross - average
    variance = jnp.mean(centred * centred, axis=0, keepdims=True)
    cross = (centred * lax.rsqrt(variance + epsilon)).astype(jnp.bfloat16)
    update = lax.dot_general(
        weight[...], cross, (((0,), (0,)), ((), ())), preferred_element_type=jnp.float32
    )
    wide[...] = (gate[...] * update).T
    lane = lax.broadcasted_iota(jnp.int32, (channels, lanes), 1)
    scores = jnp.zeros((columns, lanes), jnp.float32)
    for i in range(rows):
        line = pair[i].astype(jnp.float32) + wide[pl.ds(i, columns, stride=rows), :]
        line = line.astype(jnp.bfloat16)
        coupling[i] = line
        normed = normed_rows(line.astype(jnp.float32)).astype(jnp.bfloat16)
        own = jnp.where(lane // heads == i, bias[...], jnp.zeros((), jnp.bfloat16))
        scores = scores + jnp.dot(normed, own, preferred_element_type=jnp.float32)
    place = lax.broadcasted_iota(jnp.int32, (columns, lanes), 0)
    first_column = lax.axis_index("col") * columns
    valid = jnp.zeros((columns, lanes), jnp.int32)
    for j in range(columns):
        valid = jnp.where(place == j, mask[first_column + j], valid)
    any_valid = jnp.max(all_valid[...], axis=1, keepdims=True)
    any_valid = jnp.max(any_valid, axis=0, keepdims=True) > 0
    scores = scores + (valid.astype(jnp.float32) - 1.0) * mask_offset
    scores = jnp.where(any_valid, jnp.maximum(scores, score_floor), scores + mask_offset)
    top = jnp.max(scores, axis=0, keepdims=True).astype(jnp.bfloat16).astype(jnp.float32)
    spread[:columns, :] = jnp.exp(scores - top)
    spread[columns:, :] = jnp.broadcast_to(top, (spread.shape[0] - columns, lanes))


def shards(
    pair_state,
    sequence_embedding,
    token_valid_mask,
    sequence_present_flags,
    triangle_input_weight,
    triangle_output_weight,
    pair_head_bias,
    sequence_entry_matrix,
    sequence_exit_matrix,
):
    rows_here, columns_here, channels = pair_state.shape
    heads = pair_head_bias.shape[1]
    value_width = sequence_exit_matrix.shape[0]
    features = sequence_entry_matrix.shape[0]
    msa_rows = sequence_embedding.shape[0]
    row_index = lax.axis_index("row")
    col_index = lax.axis_index("col")
    row_size = lax.axis_size("row")
    col_size = lax.axis_size("col")
    fanout = row_size // col_size
    tokens = row_size * rows_here
    patch = rows_here * columns_here
    channels_here = channels // row_size
    left_parts = col_size // channels_here // fanout
    left_width = tokens // left_parts
    right_width = tokens // fanout
    moves = []
    for row in range(row_size):
        for col in range(col_size):
            target = ((row % fanout) * col_size + col) * col_size + row // fanout
            moves.append((row * col_size + col, target))

    vmem = pl.BlockSpec(memory_space=pltpu.VMEM)
    smem = pl.BlockSpec(memory_space=pltpu.SMEM)
    sent, out_gate = pl.pallas_call(
        functools.partial(project_kernel, row_size),
        out_shape=(
            jax.ShapeDtypeStruct((2 * channels, patch), jnp.bfloat16),
            jax.ShapeDtypeStruct((channels, patch), jnp.float32),
        ),
        in_specs=[pl.BlockSpec(memory_space=pltpu.HBM)] * 3,
        out_specs=(vmem, vmem),
        scratch_shapes=[
            pltpu.SMEM(token_valid_mask.shape, jnp.int32),
            pltpu.VMEM(pair_state.shape, jnp.bfloat16),
            pltpu.VMEM(triangle_input_weight.shape, jnp.bfloat16),
            pltpu.VMEM((patch, channels), jnp.float32),
            pltpu.VMEM((2 * channels, patch), jnp.float32),
            pltpu.SemaphoreType.DMA((3,)),
        ],
        compiler_params=pltpu.CompilerParams(vmem_limit_bytes=63 * 1024 * 1024),
        cost_estimate=pl.CostEstimate(
            flops=10 * patch * channels * channels, bytes_accessed=2**20, transcendentals=0
        ),
    )(token_valid_mask, pair_state, triangle_input_weight)

    got = exchange(sent.reshape(row_size, 2 * channels_here, patch), "row")
    got = got.reshape(row_size, 2, channels_here, columns_here, rows_here)
    got = jnp.transpose(got, (1, 2, 3, 0, 4))
    left = jnp.transpose(
        got[0].reshape(channels_here, columns_here, left_parts, left_width), (0, 2, 1, 3)
    ).reshape(channels_here, left_parts, 1, columns_here, left_width)
    right = jnp.transpose(
        got[1].reshape(channels_here, columns_here, col_size, fanout, rows_here), (0, 3, 1, 2, 4)
    ).reshape(channels_here, 1, fanout, columns_here, right_width)
    lead = (channels_here, left_parts, fanout, columns_here)
    sent = jnp.concatenate(
        [jnp.broadcast_to(left, lead + (left_width,)), jnp.broadcast_to(right, lead + (right_width,))],
        axis=4,
    ).reshape(col_size, columns_here, left_width + right_width)
    rider = jnp.tile(
        sequence_embedding.reshape(2, -1, left_width + right_width), (col_size // 2, 1, 1)
    )
    got = exchange(jnp.concatenate([sent, rider], axis=1), "col")
    half = got[:, columns_here:]
    half_other = lax.ppermute(half, "col", [(a, a ^ 1) for a in range(col_size)])
    first = col_index % 2 == 0
    sequence_all = jnp.concatenate(
        [jnp.where(first, half, half_other), jnp.where(first, half_other, half)], axis=1
    ).reshape(col_size, msa_rows, columns_here, features)
    got = got[:, :columns_here].reshape(tokens, left_width + right_width)
    crossed = jnp.einsum(
        "kj,ki->ji",
        got[:, left_width:],
        got[:, :left_width],
        preferred_element_type=jnp.float32,
    ).astype(jnp.bfloat16)
    got = exchange(crossed.reshape(col_size, rows_here, left_width), "col").reshape(
        channels_here, left_parts, fanout, rows_here, row_size // left_parts, rows_here
    )
    sent = jnp.transpose(got, (1, 4, 0, 2, 3, 5)).reshape(row_size, channels_here, patch)
    crossed = exchange(sent, "row").reshape(channels, patch)
    coupling_refreshed, sent = pl.pallas_call(
        update_kernel,
        out_shape=(
            jax.ShapeDtypeStruct(pair_state.shape, jnp.bfloat16),
            jax.ShapeDtypeStruct((columns_here + 8, rows_here * heads), jnp.float32),
        ),
        in_specs=[smem] + [vmem] * 6,
        out_specs=(vmem, vmem),
        scratch_shapes=[pltpu.VMEM((patch, channels), jnp.float32)],
        compiler_params=pltpu.CompilerParams(vmem_limit_bytes=32 * 1024 * 1024),
        cost_estimate=pl.CostEstimate(
            flops=4 * patch * channels * channels, bytes_accessed=2**20, transcendentals=0
        ),
    )(
        token_valid_mask,
        token_valid_mask.reshape(4, -1),
        crossed,
        out_gate,
        pair_state,
        triangle_output_weight,
        jnp.tile(pair_head_bias, (1, rows_here)),
    )
    sent = sent.astype(jnp.bfloat16)

    sent = lax.ppermute(sent, ("row", "col"), moves)
    groups = [[m * col_size + b for b in range(col_size)] for m in range(fanout)]
    mine = lax.all_to_all(
        jnp.broadcast_to(sent[None], (col_size,) + sent.shape),
        "row",
        split_axis=0,
        concat_axis=0,
        axis_index_groups=groups,
        tiled=True,
    )
    swap = [(a, (a + col_size) % row_size) for a in range(row_size)]
    other = lax.ppermute(mine, "row", swap)

    sequence_all = apply_layer_norm(sequence_all.astype(jnp.float32), 3).astype(jnp.bfloat16)
    values = jnp.einsum(
        "qsjf,fg->qjsg",
        sequence_all,
        sequence_entry_matrix[:, :value_width],
        preferred_element_type=jnp.float32,
    ).astype(jnp.bfloat16).reshape(tokens, msa_rows * value_width)
    own = (
        lax.broadcasted_iota(jnp.int32, (heads, 1, value_width), 2) // (value_width // heads)
        == lax.broadcasted_iota(jnp.int32, (heads, 1, value_width), 0)
    )

    def average(got):
        got = got.astype(jnp.float32)
        tops = got[:, columns_here : columns_here + 1]
        exponent = got[:, :columns_here] * jnp.exp(tops - jnp.max(tops, axis=0, keepdims=True))
        weights = (exponent / jnp.sum(exponent, axis=(0, 1), keepdims=True)).astype(jnp.bfloat16)
        averaged = jnp.einsum(
            "jp,jx->px",
            weights.reshape(tokens, rows_here * heads),
            values,
            preferred_element_type=jnp.float32,
        ).reshape(rows_here, heads, msa_rows, value_width)
        return jnp.sum(jnp.where(own[None], averaged, 0.0), axis=1)

    mine = average(mine)
    other = average(other)
    low = row_index < col_size
    averaged = jnp.concatenate(
        [jnp.where(low, mine, other), jnp.where(low, other, mine)], axis=0
    )
    sequence_slab = sequence_embedding.reshape(msa_rows, columns_here, features).astype(jnp.float32)
    sequence_normed = apply_layer_norm(sequence_slab, 2).astype(jnp.bfloat16)
    sequence_switch = jax.nn.sigmoid(
        jnp.einsum(
            "sjf,fg->jsg",
            sequence_normed,
            sequence_entry_matrix[:, value_width:],
            preferred_element_type=jnp.float32,
        )
    )
    switched = (sequence_switch * averaged).astype(jnp.bfloat16)
    final_output = jnp.einsum(
        "isg,gf->sif", switched, sequence_exit_matrix, preferred_element_type=jnp.float32
    )
    sequence_refreshed = (
        sequence_slab + sequence_present_flags.astype(jnp.float32)[:, None, None] * final_output
    ).astype(jnp.bfloat16)
    return (
        coupling_refreshed,
        sequence_refreshed.reshape(msa_rows, columns_here * features),
    )


def solution(mesh):
    placed = (P("row", "col", None), P("row", "col"), P(), P("row"), P(), P(), P(), P(), P())
    return jax.shard_map(
        shards,
        mesh=mesh,
        in_specs=placed,
        out_specs=(P("row", "col", None), P("row", "col")),
        check_vma=False,
    )
```

```python
import functools

import jax
import jax.numpy as jnp
import numpy as np
from jax import lax
from jax.experimental import pallas as pl
from jax.experimental.pallas import tpu as pltpu
from jax.sharding import PartitionSpec as P

epsilon = 1e-05
mask_offset = 1000000000.0
score_floor = -8192.0


def apply_layer_norm(array, along):
    average = jnp.mean(array, axis=along, keepdims=True)
    centred = array - average
    spread = jnp.mean(centred * centred, axis=along, keepdims=True)
    return centred * lax.rsqrt(spread + epsilon)


def exchange(blocks, axis):
    return lax.all_to_all(blocks, axis, split_axis=0, concat_axis=0, tiled=True)


def normed_rows(array):
    average = jnp.mean(array, axis=-1, keepdims=True)
    centred = array - average
    spread = jnp.mean(centred * centred, axis=-1, keepdims=True)
    return centred * lax.rsqrt(spread + epsilon)


def project_kernel(
    row_size, mask_far, pair_far, weight_far, sent, gate, mask, pair, weight, wide, mixed, arrived
):
    copies = [
        pltpu.make_async_copy(pair_far, pair, arrived.at[0]),
        pltpu.make_async_copy(weight_far, weight, arrived.at[1]),
        pltpu.make_async_copy(mask_far, mask, arrived.at[2]),
    ]
    for copy in copies:
        copy.start()
    for copy in copies:
        copy.wait()
    rows, columns, channels = pair.shape
    patch = rows * columns
    here = channels // row_size
    wide[...] = normed_rows(pair[...].astype(jnp.float32).reshape(patch, channels))
    normed = jnp.concatenate(
        [wide[pl.ds(k, rows, stride=columns), :] for k in range(columns)], axis=0
    ).astype(jnp.bfloat16)
    projected = lax.dot_general(
        weight[...], normed, (((0,), (1,)), ((), ())), preferred_element_type=jnp.float32
    )
    lane = lax.broadcasted_iota(jnp.int32, (1, patch), 1)
    first_row = lax.axis_index("row") * rows
    first_column = lax.axis_index("col") * columns
    row_valid = jnp.zeros((1, patch), jnp.int32)
    column_valid = jnp.zeros((1, patch), jnp.int32)
    for i in range(rows):
        row_valid = jnp.where(lane % rows == i, mask[first_row + i], row_valid)
    for k in range(columns):
        column_valid = jnp.where(lane // rows == k, mask[first_column + k], column_valid)
    valid = (row_valid * column_valid).astype(jnp.float32)
    left = jax.nn.sigmoid(projected[:channels]) * projected[channels : 2 * channels] * valid
    right = (
        jax.nn.sigmoid(projected[2 * channels : 3 * channels])
        * projected[3 * channels : 4 * channels]
        * valid
    )
    gate[...] = jax.nn.sigmoid(projected[4 * channels :])
    for r in range(row_size):
        mixed[2 * r * here : (2 * r + 1) * here, :] = left[r * here : (r + 1) * here]
        mixed[(2 * r + 1) * here : (2 * r + 2) * here, :] = right[r * here : (r + 1) * here]
    sent[...] = mixed[...].astype(jnp.bfloat16)


def update_kernel(mask, all_valid, crossed, gate, pair, weight, bias, coupling, spread, wide):
    rows, columns, channels = pair.shape
    patch = rows * columns
    lanes = bias.shape[1]
    heads = lanes // rows
    cross = crossed[...].astype(jnp.float32)
    average = jnp.mean(cross, axis=0, keepdims=True)
    centred = cross - average
    variance = jnp.mean(centred * centred, axis=0, keepdims=True)
    cross = (centred * lax.rsqrt(variance + epsilon)).astype(jnp.bfloat16)
    update = lax.dot_general(
        weight[...], cross, (((0,), (0,)), ((), ())), preferred_element_type=jnp.float32
    )
    wide[...] = (gate[...] * update).T
    lane = lax.broadcasted_iota(jnp.int32, (channels, lanes), 1)
    scores = jnp.zeros((columns, lanes), jnp.float32)
    for i in range(rows):
        line = pair[i].astype(jnp.float32) + wide[pl.ds(i, columns, stride=rows), :]
        line = line.astype(jnp.bfloat16)
        coupling[i] = line
        normed = normed_rows(line.astype(jnp.float32)).astype(jnp.bfloat16)
        own = jnp.where(lane // heads == i, bias[...], jnp.zeros((), jnp.bfloat16))
        scores = scores + jnp.dot(normed, own, preferred_element_type=jnp.float32)
    place = lax.broadcasted_iota(jnp.int32, (columns, lanes), 0)
    first_column = lax.axis_index("col") * columns
    valid = jnp.zeros((columns, lanes), jnp.int32)
    for j in range(columns):
        valid = jnp.where(place == j, mask[first_column + j], valid)
    any_valid = jnp.max(all_valid[...], axis=1, keepdims=True)
    any_valid = jnp.max(any_valid, axis=0, keepdims=True) > 0
    scores = scores + (valid.astype(jnp.float32) - 1.0) * mask_offset
    scores = jnp.where(any_valid, jnp.maximum(scores, score_floor), scores + mask_offset)
    top = jnp.max(scores, axis=0, keepdims=True).astype(jnp.bfloat16).astype(jnp.float32)
    spread[:columns, :] = jnp.exp(scores - top)
    spread[columns:, :] = jnp.broadcast_to(top, (spread.shape[0] - columns, lanes))


def average_kernel(value_width, places, got, values, averaged, wide, ordered):
    blocks, deep, lanes = got.shape
    columns = deep - 8
    rows, across = averaged.shape
    heads = lanes // rows
    wide[...] = got[...].astype(jnp.float32)
    top = jnp.max(wide[:, columns : columns + 1, :], axis=0)
    total = jnp.zeros((1, lanes), jnp.float32)
    for block in range(blocks):
        place = places[block]
        factor = jnp.exp(wide[place, columns : columns + 1, :] - top)
        piece = wide[place, :columns, :] * factor
        total = total + jnp.sum(piece, axis=0, keepdims=True)
        ordered[block * columns : (block + 1) * columns, :] = piece
    weights = (ordered[...] / total).astype(jnp.bfloat16)
    own = lax.broadcasted_iota(jnp.int32, (lanes, value_width), 0) % heads == (
        lax.broadcasted_iota(jnp.int32, (lanes, value_width), 1) // (value_width // heads)
    )
    for start in range(0, across, value_width):
        product = lax.dot_general(
            weights,
            values[:, start : start + value_width],
            (((0,), (0,)), ((), ())),
            preferred_element_type=jnp.float32,
        )
        product = jnp.where(own, product, 0.0).reshape(rows, heads, value_width)
        averaged[:, start : start + value_width] = jnp.sum(product, axis=1)


def ring(a, b, size):
    return min((a - b) % size, (b - a) % size)


def score_places(row_size, col_size):
    around = col_size // 4
    offsets = sorted(range(-(col_size // 2) + 1, col_size // 2 + 1), key=abs)
    places = np.zeros((col_size, 2, col_size), np.int32)
    for row in range(row_size):
        to_col, to_x = row // 2, row % 2

        def far(col):
            x = ring(2 * (col // (col_size // 2)) + row // col_size,
                     2 * (to_col // (col_size // 2)) + to_x, 4)
            return x + ring(col // 2 % around, to_col // 2 % around, around) + (col ^ to_col) % 2

        order = sorted(range(col_size), key=far, reverse=True)
        for offset, col in zip(offsets, order):
            places[to_col, to_x, col] = (row + offset) % col_size
    return places


def shards(
    pair_state,
    sequence_embedding,
    token_valid_mask,
    sequence_present_flags,
    triangle_input_weight,
    triangle_output_weight,
    pair_head_bias,
    sequence_entry_matrix,
    sequence_exit_matrix,
):
    rows_here, columns_here, channels = pair_state.shape
    heads = pair_head_bias.shape[1]
    value_width = sequence_exit_matrix.shape[0]
    features = sequence_entry_matrix.shape[0]
    msa_rows = sequence_embedding.shape[0]
    row_index = lax.axis_index("row")
    col_index = lax.axis_index("col")
    row_size = lax.axis_size("row")
    col_size = lax.axis_size("col")
    fanout = row_size // col_size
    tokens = row_size * rows_here
    patch = rows_here * columns_here
    channels_here = channels // row_size
    left_parts = col_size // channels_here // fanout
    left_width = tokens // left_parts
    right_width = tokens // fanout
    places = score_places(row_size, col_size)
    moves = []
    for row in range(row_size):
        for col in range(col_size):
            to_row = row % fanout * col_size + int(places[row // fanout, row % fanout, col])
            moves.append((row * col_size + col, to_row * col_size + row // fanout))

    vmem = pl.BlockSpec(memory_space=pltpu.VMEM)
    smem = pl.BlockSpec(memory_space=pltpu.SMEM)
    sent, out_gate = pl.pallas_call(
        functools.partial(project_kernel, row_size),
        out_shape=(
            jax.ShapeDtypeStruct((2 * channels, patch), jnp.bfloat16),
            jax.ShapeDtypeStruct((channels, patch), jnp.float32),
        ),
        in_specs=[pl.BlockSpec(memory_space=pltpu.HBM)] * 3,
        out_specs=(vmem, vmem),
        scratch_shapes=[
            pltpu.SMEM(token_valid_mask.shape, jnp.int32),
            pltpu.VMEM(pair_state.shape, jnp.bfloat16),
            pltpu.VMEM(triangle_input_weight.shape, jnp.bfloat16),
            pltpu.VMEM((patch, channels), jnp.float32),
            pltpu.VMEM((2 * channels, patch), jnp.float32),
            pltpu.SemaphoreType.DMA((3,)),
        ],
        compiler_params=pltpu.CompilerParams(vmem_limit_bytes=63 * 1024 * 1024),
        cost_estimate=pl.CostEstimate(
            flops=10 * patch * channels * channels, bytes_accessed=2**20, transcendentals=0
        ),
    )(token_valid_mask, pair_state, triangle_input_weight)

    got = exchange(sent.reshape(row_size, 2 * channels_here, patch), "row")
    got = got.reshape(row_size, 2, channels_here, columns_here, rows_here)
    got = jnp.transpose(got, (1, 2, 3, 0, 4))
    left = jnp.transpose(
        got[0].reshape(channels_here, columns_here, left_parts, left_width), (0, 2, 1, 3)
    ).reshape(channels_here, left_parts, 1, columns_here, left_width)
    right = jnp.transpose(
        got[1].reshape(channels_here, columns_here, col_size, fanout, rows_here), (0, 3, 1, 2, 4)
    ).reshape(channels_here, 1, fanout, columns_here, right_width)
    lead = (channels_here, left_parts, fanout, columns_here)
    sent = jnp.concatenate(
        [jnp.broadcast_to(left, lead + (left_width,)), jnp.broadcast_to(right, lead + (right_width,))],
        axis=4,
    ).reshape(col_size, columns_here, left_width + right_width)
    rider = jnp.tile(
        sequence_embedding.reshape(2, -1, left_width + right_width), (col_size // 2, 1, 1)
    )
    got = exchange(jnp.concatenate([sent, rider], axis=1), "col")
    half = got[:, columns_here:]
    half_other = lax.ppermute(half, "col", [(a, a ^ 1) for a in range(col_size)])
    first = col_index % 2 == 0
    sequence_all = jnp.concatenate(
        [jnp.where(first, half, half_other), jnp.where(first, half_other, half)], axis=1
    ).reshape(col_size, msa_rows, columns_here, features)
    got = got[:, :columns_here].reshape(tokens, left_width + right_width)
    crossed = jnp.einsum(
        "kj,ki->ji",
        got[:, left_width:],
        got[:, :left_width],
        preferred_element_type=jnp.float32,
    ).astype(jnp.bfloat16)
    got = exchange(crossed.reshape(col_size, rows_here, left_width), "col").reshape(
        channels_here, left_parts, fanout, rows_here, row_size // left_parts, rows_here
    )
    sent = jnp.transpose(got, (1, 4, 0, 2, 3, 5)).reshape(row_size, channels_here, patch)
    crossed = exchange(sent, "row").reshape(channels, patch)
    coupling_refreshed, sent = pl.pallas_call(
        update_kernel,
        out_shape=(
            jax.ShapeDtypeStruct(pair_state.shape, jnp.bfloat16),
            jax.ShapeDtypeStruct((columns_here + 8, rows_here * heads), jnp.float32),
        ),
        in_specs=[smem] + [vmem] * 6,
        out_specs=(vmem, vmem),
        scratch_shapes=[pltpu.VMEM((patch, channels), jnp.float32)],
        compiler_params=pltpu.CompilerParams(vmem_limit_bytes=32 * 1024 * 1024),
        cost_estimate=pl.CostEstimate(
            flops=4 * patch * channels * channels, bytes_accessed=2**20, transcendentals=0
        ),
    )(
        token_valid_mask,
        token_valid_mask.reshape(4, -1),
        crossed,
        out_gate,
        pair_state,
        triangle_output_weight,
        jnp.tile(pair_head_bias, (1, rows_here)),
    )
    sent = sent.astype(jnp.bfloat16)

    sent = lax.ppermute(sent, ("row", "col"), moves)
    groups = [[m * col_size + b for b in range(col_size)] for m in range(fanout)]
    mine = lax.all_to_all(
        jnp.broadcast_to(sent[None], (col_size,) + sent.shape),
        "row",
        split_axis=0,
        concat_axis=0,
        axis_index_groups=groups,
        tiled=True,
    )
    swap = [(a, (a + col_size) % row_size) for a in range(row_size)]
    other = lax.ppermute(mine, "row", swap)

    sequence_all = apply_layer_norm(sequence_all.astype(jnp.float32), 3).astype(jnp.bfloat16)
    values = jnp.einsum(
        "qsjf,fg->qjsg",
        sequence_all,
        sequence_entry_matrix[:, :value_width],
        preferred_element_type=jnp.float32,
    ).astype(jnp.bfloat16).reshape(tokens, msa_rows * value_width)
    places = lax.dynamic_index_in_dim(jnp.asarray(places), col_index, 0, keepdims=False)
    half_index = row_index // col_size

    def average(got, which):
        return pl.pallas_call(
            functools.partial(average_kernel, value_width),
            out_shape=jax.ShapeDtypeStruct((rows_here, msa_rows * value_width), jnp.float32),
            in_specs=[smem, vmem, vmem],
            out_specs=vmem,
            scratch_shapes=[
                pltpu.VMEM(got.shape, jnp.float32),
                pltpu.VMEM((tokens, rows_here * heads), jnp.float32),
            ],
            compiler_params=pltpu.CompilerParams(vmem_limit_bytes=32 * 1024 * 1024),
            cost_estimate=pl.CostEstimate(
                flops=2 * tokens * rows_here * heads * msa_rows * value_width,
                bytes_accessed=3 * 2**20,
                transcendentals=0,
            ),
        )(
            lax.dynamic_index_in_dim(places, which, 0, keepdims=False), got, values
        ).reshape(rows_here, msa_rows, value_width)

    mine = average(mine, half_index)
    other = average(other, 1 - half_index)
    low = row_index < col_size
    averaged = jnp.concatenate(
        [jnp.where(low, mine, other), jnp.where(low, other, mine)], axis=0
    )
    sequence_slab = sequence_embedding.reshape(msa_rows, columns_here, features).astype(jnp.float32)
    sequence_normed = apply_layer_norm(sequence_slab, 2).astype(jnp.bfloat16)
    sequence_switch = jax.nn.sigmoid(
        jnp.einsum(
            "sjf,fg->jsg",
            sequence_normed,
            sequence_entry_matrix[:, value_width:],
            preferred_element_type=jnp.float32,
        )
    )
    switched = (sequence_switch * averaged).astype(jnp.bfloat16)
    final_output = jnp.einsum(
        "isg,gf->sif", switched, sequence_exit_matrix, preferred_element_type=jnp.float32
    )
    sequence_refreshed = (
        sequence_slab + sequence_present_flags.astype(jnp.float32)[:, None, None] * final_output
    ).astype(jnp.bfloat16)
    return (
        coupling_refreshed,
        sequence_refreshed.reshape(msa_rows, columns_here * features),
    )


def solution(mesh):
    placed = (P("row", "col", None), P("row", "col"), P(), P("row"), P(), P(), P(), P(), P())
    return jax.shard_map(
        shards,
        mesh=mesh,
        in_specs=placed,
        out_specs=(P("row", "col", None), P("row", "col")),
        check_vma=False,
    )
```

```python
import functools

import jax
import jax.numpy as jnp
import numpy as np
from jax import lax
from jax.experimental import pallas as pl
from jax.experimental.pallas import tpu as pltpu
from jax.sharding import PartitionSpec as P

epsilon = 1e-05
mask_offset = 1000000000.0
score_floor = -8192.0


def apply_layer_norm(array, along):
    average = jnp.mean(array, axis=along, keepdims=True)
    centred = array - average
    spread = jnp.mean(centred * centred, axis=along, keepdims=True)
    return centred * lax.rsqrt(spread + epsilon)


def exchange(blocks, axis):
    return lax.all_to_all(blocks, axis, split_axis=0, concat_axis=0, tiled=True)


def normed_rows(array):
    average = jnp.mean(array, axis=-1, keepdims=True)
    centred = array - average
    spread = jnp.mean(centred * centred, axis=-1, keepdims=True)
    return centred * lax.rsqrt(spread + epsilon)


def project_kernel(
    row_size, mask_far, pair_far, weight_far, sent, gate, mask, pair, weight, mixed, arrived
):
    copies = [
        pltpu.make_async_copy(pair_far, pair, arrived.at[0]),
        pltpu.make_async_copy(weight_far, weight, arrived.at[1]),
        pltpu.make_async_copy(mask_far, mask, arrived.at[2]),
    ]
    for copy in copies:
        copy.start()
    for copy in copies:
        copy.wait()
    rows, columns, channels = pair.shape
    patch = rows * columns
    here = channels // row_size
    normed = normed_rows(pair[...].astype(jnp.float32).reshape(patch, channels))
    normed = normed.astype(jnp.bfloat16)
    projected = lax.dot_general(
        weight[:, : 4 * channels],
        normed,
        (((0,), (1,)), ((), ())),
        preferred_element_type=jnp.float32,
    )
    lane = lax.broadcasted_iota(jnp.int32, (1, patch), 1)
    first_row = lax.axis_index("row") * rows
    first_column = lax.axis_index("col") * columns
    row_valid = jnp.zeros((1, patch), jnp.int32)
    column_valid = jnp.zeros((1, patch), jnp.int32)
    for i in range(rows):
        row_valid = jnp.where(lane // columns == i, mask[first_row + i], row_valid)
    for k in range(columns):
        column_valid = jnp.where(lane % columns == k, mask[first_column + k], column_valid)
    valid = (row_valid * column_valid).astype(jnp.float32)
    left = jax.nn.sigmoid(projected[:channels]) * projected[channels : 2 * channels] * valid
    right = (
        jax.nn.sigmoid(projected[2 * channels : 3 * channels])
        * projected[3 * channels : 4 * channels]
        * valid
    )
    for r in range(row_size):
        mixed[2 * r * here : (2 * r + 1) * here, :] = left[r * here : (r + 1) * here]
        mixed[(2 * r + 1) * here : (2 * r + 2) * here, :] = right[r * here : (r + 1) * here]
    sent[...] = mixed[...].astype(jnp.bfloat16)
    gate[...] = jax.nn.sigmoid(
        jnp.dot(normed, weight[:, 4 * channels :], preferred_element_type=jnp.float32)
    )


def tiled(rows, lanes):
    return lanes // min(lanes, 128), rows, min(lanes, 128)


def put_tiles(ref, value, rows=slice(None)):
    for tile in range(ref.shape[0]):
        ref[tile, rows, :] = value[:, tile * ref.shape[2] : (tile + 1) * ref.shape[2]]


def get_tiles(ref, rows):
    return jnp.concatenate([ref[tile, rows, :] for tile in range(ref.shape[0])], axis=1)


def regroup(pieces, here):
    lanes = pieces[0].shape[1]
    step = lanes // here
    group = lax.broadcasted_iota(jnp.int32, pieces[0].shape, 1) // step
    results = []
    for c in range(here):
        tiles = []
        for first in range(0, len(pieces), here):
            tile = pieces[first + c]
            for n in range(here):
                if n != c:
                    moved = pltpu.roll(pieces[first + n], (n - c) % here * step, axis=1)
                    tile = jnp.where(group == n, moved, tile)
            tiles.append(tile)
        results.append(jnp.concatenate(tiles, axis=1))
    return results


def gathered_kernel(columns, got, rider, sent, wide, turned):
    row_size, double, patch = got.shape
    here = double // 2
    rows = patch // columns
    put_tiles(wide, got[...].astype(jnp.float32).reshape(row_size * double, patch))
    sides = []
    for side in range(2):
        stacked = jnp.concatenate(
            [get_tiles(wide, pl.ds(side * here + c, row_size, stride=double)) for c in range(here)],
            axis=0,
        )
        turned[...] = stacked.T
        pieces = [turned[t * columns : (t + 1) * columns, :] for t in range(rows)]
        sides.append(
            [[block.astype(jnp.bfloat16) for block in regroup(pieces[h : h + rows // 2], here)]
             for h in (0, rows // 2)]
        )
    width = rows // 2 * row_size
    for c in range(here):
        for i in range(2):
            for j in range(2):
                place = (c * 2 + i) * 2 + j
                sent[place, :columns, :width] = sides[0][i][c]
                sent[place, :columns, width:] = sides[1][j][c]
                sent[place, columns:, :] = rider[place % 2]


def multiply_kernel(columns, row_size, got, crossed, wide):
    blocks = got.shape[0]
    width = got.shape[2] // 2
    both = jnp.concatenate([got[q, :columns, :] for q in range(blocks)], axis=0)
    product = lax.dot_general(
        both[:, width:], both[:, :width], (((0,), (0,)), ((), ())), preferred_element_type=jnp.float32
    )
    put_tiles(wide, product)
    half = width // row_size
    for q in range(blocks):
        crossed[q] = jnp.concatenate(
            [get_tiles(wide, pl.ds(2 * q + m, half, stride=row_size)) for m in range(2)], axis=0
        ).astype(jnp.bfloat16)


def returned_kernel(here, row_size, got, sent, wide):
    half = got.shape[1] // 2
    pieces = []
    for i in range(2):
        stacked = []
        for c in range(here):
            for m in range(2):
                for j in range(2):
                    place = (c * 2 + i) * 2 + j
                    stacked.append(got[place].astype(jnp.float32)[m * half : (m + 1) * half])
        turned = jnp.concatenate(stacked, axis=0).T
        pieces += [turned[t * row_size : (t + 1) * row_size] for t in range(half)]
    for c, block in enumerate(regroup(pieces, here)):
        put_tiles(wide, block, pl.ds(c, row_size, stride=here))
    sent[...] = get_tiles(wide, slice(None)).astype(jnp.bfloat16)


def update_kernel(columns, mask, all_valid, crossed, gate, pair, weight, bias, coupling, spread):
    patch, channels = pair.shape
    rows = patch // columns
    lanes = bias.shape[1]
    heads = lanes // rows
    cross = crossed[...].astype(jnp.float32)
    average = jnp.mean(cross, axis=0, keepdims=True)
    centred = cross - average
    variance = jnp.mean(centred * centred, axis=0, keepdims=True)
    cross = (centred * lax.rsqrt(variance + epsilon)).astype(jnp.bfloat16)
    update = lax.dot_general(
        cross, weight[...], (((0,), (0,)), ((), ())), preferred_element_type=jnp.float32
    )
    after = (pair[...].astype(jnp.float32) + gate[...] * update).astype(jnp.bfloat16)
    coupling[...] = after
    normed = normed_rows(after.astype(jnp.float32)).astype(jnp.bfloat16)
    lane = lax.broadcasted_iota(jnp.int32, (channels, lanes), 1)
    scores = jnp.zeros((columns, lanes), jnp.float32)
    for i in range(rows):
        own = jnp.where(lane // heads == i, bias[...], jnp.zeros((), jnp.bfloat16))
        scores = scores + jnp.dot(
            normed[i * columns : (i + 1) * columns], own, preferred_element_type=jnp.float32
        )
    place = lax.broadcasted_iota(jnp.int32, (columns, lanes), 0)
    first_column = lax.axis_index("col") * columns
    valid = jnp.zeros((columns, lanes), jnp.int32)
    for j in range(columns):
        valid = jnp.where(place == j, mask[first_column + j], valid)
    any_valid = jnp.max(all_valid[...], axis=1, keepdims=True)
    any_valid = jnp.max(any_valid, axis=0, keepdims=True) > 0
    scores = scores + (valid.astype(jnp.float32) - 1.0) * mask_offset
    scores = jnp.where(any_valid, jnp.maximum(scores, score_floor), scores + mask_offset)
    top = jnp.max(scores, axis=0, keepdims=True).astype(jnp.bfloat16).astype(jnp.float32)
    spread[:columns, :] = jnp.exp(scores - top)
    spread[columns:, :] = jnp.broadcast_to(top, (spread.shape[0] - columns, lanes))


def average_kernel(value_width, places, got, values, averaged, wide, ordered):
    blocks, deep, lanes = got.shape
    columns = deep - 8
    rows, across = averaged.shape
    heads = lanes // rows
    wide[...] = got[...].astype(jnp.float32)
    top = jnp.max(wide[:, columns : columns + 1, :], axis=0)
    total = jnp.zeros((1, lanes), jnp.float32)
    for block in range(blocks):
        place = places[block]
        factor = jnp.exp(wide[place, columns : columns + 1, :] - top)
        piece = wide[place, :columns, :] * factor
        total = total + jnp.sum(piece, axis=0, keepdims=True)
        ordered[block * columns : (block + 1) * columns, :] = piece
    weights = (ordered[...] / total).astype(jnp.bfloat16)
    own = lax.broadcasted_iota(jnp.int32, (lanes, value_width), 0) % heads == (
        lax.broadcasted_iota(jnp.int32, (lanes, value_width), 1) // (value_width // heads)
    )
    for start in range(0, across, value_width):
        product = lax.dot_general(
            weights,
            values[:, start : start + value_width],
            (((0,), (0,)), ((), ())),
            preferred_element_type=jnp.float32,
        )
        product = jnp.where(own, product, 0.0).reshape(rows, heads, value_width)
        averaged[:, start : start + value_width] = jnp.sum(product, axis=1)


def ring(a, b, size):
    return min((a - b) % size, (b - a) % size)


def score_places(row_size, col_size):
    around = col_size // 4
    offsets = sorted(range(-(col_size // 2) + 1, col_size // 2 + 1), key=abs)
    places = np.zeros((col_size, 2, col_size), np.int32)
    for row in range(row_size):
        to_col, to_x = row // 2, row % 2

        def far(col):
            x = ring(2 * (col // (col_size // 2)) + row // col_size,
                     2 * (to_col // (col_size // 2)) + to_x, 4)
            return x + ring(col // 2 % around, to_col // 2 % around, around) + (col ^ to_col) % 2

        order = sorted(range(col_size), key=far, reverse=True)
        for offset, col in zip(offsets, order):
            places[to_col, to_x, col] = (row + offset) % col_size
    return places


def shards(
    pair_state,
    sequence_embedding,
    token_valid_mask,
    sequence_present_flags,
    triangle_input_weight,
    triangle_output_weight,
    pair_head_bias,
    sequence_entry_matrix,
    sequence_exit_matrix,
):
    rows_here, columns_here, channels = pair_state.shape
    heads = pair_head_bias.shape[1]
    value_width = sequence_exit_matrix.shape[0]
    features = sequence_entry_matrix.shape[0]
    msa_rows = sequence_embedding.shape[0]
    row_index = lax.axis_index("row")
    col_index = lax.axis_index("col")
    row_size = lax.axis_size("row")
    col_size = lax.axis_size("col")
    fanout = row_size // col_size
    tokens = row_size * rows_here
    patch = rows_here * columns_here
    channels_here = channels // row_size
    width = tokens // 2
    places = score_places(row_size, col_size)
    moves = []
    for row in range(row_size):
        for col in range(col_size):
            to_row = row % fanout * col_size + int(places[row // fanout, row % fanout, col])
            moves.append((row * col_size + col, to_row * col_size + row // fanout))

    vmem = pl.BlockSpec(memory_space=pltpu.VMEM)
    smem = pl.BlockSpec(memory_space=pltpu.SMEM)
    spacious = pltpu.CompilerParams(vmem_limit_bytes=32 * 1024 * 1024)

    def work(flops):
        return pl.CostEstimate(flops=flops, bytes_accessed=2**20, transcendentals=0)

    sent, out_gate = pl.pallas_call(
        functools.partial(project_kernel, row_size),
        out_shape=(
            jax.ShapeDtypeStruct((2 * channels, patch), jnp.bfloat16),
            jax.ShapeDtypeStruct((patch, channels), jnp.float32),
        ),
        in_specs=[pl.BlockSpec(memory_space=pltpu.HBM)] * 3,
        out_specs=(vmem, vmem),
        scratch_shapes=[
            pltpu.SMEM(token_valid_mask.shape, jnp.int32),
            pltpu.VMEM(pair_state.shape, jnp.bfloat16),
            pltpu.VMEM(triangle_input_weight.shape, jnp.bfloat16),
            pltpu.VMEM((2 * channels, patch), jnp.float32),
            pltpu.SemaphoreType.DMA((3,)),
        ],
        compiler_params=pltpu.CompilerParams(vmem_limit_bytes=63 * 1024 * 1024),
        cost_estimate=work(10 * patch * channels * channels),
    )(token_valid_mask, pair_state, triangle_input_weight)

    got = exchange(sent.reshape(row_size, 2 * channels_here, patch), "row")
    rider = sequence_embedding.reshape(2, -1, 2 * width)
    sent = pl.pallas_call(
        functools.partial(gathered_kernel, columns_here),
        out_shape=jax.ShapeDtypeStruct(
            (col_size, columns_here + rider.shape[1], 2 * width), jnp.bfloat16
        ),
        in_specs=[vmem, vmem],
        out_specs=vmem,
        scratch_shapes=[
            pltpu.VMEM(tiled(2 * channels, patch), jnp.float32),
            pltpu.VMEM((patch, channels), jnp.float32),
        ],
        compiler_params=spacious,
        cost_estimate=work(patch * channels),
    )(got, rider)
    got = exchange(sent, "col")
    half = got[:, columns_here:]
    half_other = lax.ppermute(half, "col", [(a, a ^ 1) for a in range(col_size)])
    first = col_index % 2 == 0
    sequence_all = jnp.concatenate(
        [jnp.where(first, half, half_other), jnp.where(first, half_other, half)], axis=1
    ).reshape(col_size, msa_rows, columns_here, features)
    sent = pl.pallas_call(
        functools.partial(multiply_kernel, columns_here, row_size),
        out_shape=jax.ShapeDtypeStruct((col_size, rows_here, width), jnp.bfloat16),
        in_specs=[vmem],
        out_specs=vmem,
        scratch_shapes=[pltpu.VMEM(tiled(width, width), jnp.float32)],
        compiler_params=spacious,
        cost_estimate=work(2 * tokens * width * width),
    )(got)
    got = exchange(sent, "col")
    sent = pl.pallas_call(
        functools.partial(returned_kernel, channels_here, row_size),
        out_shape=jax.ShapeDtypeStruct((channels, patch), jnp.bfloat16),
        in_specs=[vmem],
        out_specs=vmem,
        scratch_shapes=[pltpu.VMEM(tiled(channels, patch), jnp.float32)],
        compiler_params=spacious,
        cost_estimate=work(patch * channels),
    )(got)
    crossed = exchange(sent.reshape(row_size, channels_here, patch), "row").reshape(channels, patch)
    coupling_refreshed, sent = pl.pallas_call(
        functools.partial(update_kernel, columns_here),
        out_shape=(
            jax.ShapeDtypeStruct((patch, channels), jnp.bfloat16),
            jax.ShapeDtypeStruct((columns_here + 8, rows_here * heads), jnp.float32),
        ),
        in_specs=[smem] + [vmem] * 6,
        out_specs=(vmem, vmem),
        compiler_params=spacious,
        cost_estimate=work(4 * patch * channels * channels),
    )(
        token_valid_mask,
        token_valid_mask.reshape(4, -1),
        crossed,
        out_gate,
        pair_state.reshape(patch, channels),
        triangle_output_weight,
        jnp.tile(pair_head_bias, (1, rows_here)),
    )
    coupling_refreshed = coupling_refreshed.reshape(rows_here, columns_here, channels)
    sent = sent.astype(jnp.bfloat16)

    sent = lax.ppermute(sent, ("row", "col"), moves)
    groups = [[m * col_size + b for b in range(col_size)] for m in range(fanout)]
    mine = lax.all_to_all(
        jnp.broadcast_to(sent[None], (col_size,) + sent.shape),
        "row",
        split_axis=0,
        concat_axis=0,
        axis_index_groups=groups,
        tiled=True,
    )
    sequence_all = apply_layer_norm(sequence_all.astype(jnp.float32), 3).astype(jnp.bfloat16)
    values = jnp.einsum(
        "qsjf,fg->qjsg",
        sequence_all,
        sequence_entry_matrix[:, :value_width],
        preferred_element_type=jnp.float32,
    ).astype(jnp.bfloat16).reshape(tokens, msa_rows * value_width)
    mine, values = lax.optimization_barrier((mine, values))
    swap = [(a, (a + col_size) % row_size) for a in range(row_size)]
    other = lax.ppermute(mine, "row", swap)

    places = lax.dynamic_index_in_dim(jnp.asarray(places), col_index, 0, keepdims=False)
    half_index = row_index // col_size

    def average(got, which):
        return pl.pallas_call(
            functools.partial(average_kernel, value_width),
            out_shape=jax.ShapeDtypeStruct((rows_here, msa_rows * value_width), jnp.float32),
            in_specs=[smem, vmem, vmem],
            out_specs=vmem,
            scratch_shapes=[
                pltpu.VMEM(got.shape, jnp.float32),
                pltpu.VMEM((tokens, rows_here * heads), jnp.float32),
            ],
            compiler_params=pltpu.CompilerParams(vmem_limit_bytes=32 * 1024 * 1024),
            cost_estimate=pl.CostEstimate(
                flops=2 * tokens * rows_here * heads * msa_rows * value_width,
                bytes_accessed=3 * 2**20,
                transcendentals=0,
            ),
        )(
            lax.dynamic_index_in_dim(places, which, 0, keepdims=False), got, values
        ).reshape(rows_here, msa_rows, value_width)

    mine = average(mine, half_index)
    other = average(other, 1 - half_index)
    low = row_index < col_size
    averaged = jnp.concatenate(
        [jnp.where(low, mine, other), jnp.where(low, other, mine)], axis=0
    )
    sequence_slab = sequence_embedding.reshape(msa_rows, columns_here, features).astype(jnp.float32)
    sequence_normed = apply_layer_norm(sequence_slab, 2).astype(jnp.bfloat16)
    sequence_switch = jax.nn.sigmoid(
        jnp.einsum(
            "sjf,fg->jsg",
            sequence_normed,
            sequence_entry_matrix[:, value_width:],
            preferred_element_type=jnp.float32,
        )
    )
    switched = (sequence_switch * averaged).astype(jnp.bfloat16)
    final_output = jnp.einsum(
        "isg,gf->sif", switched, sequence_exit_matrix, preferred_element_type=jnp.float32
    )
    sequence_refreshed = (
        sequence_slab + sequence_present_flags.astype(jnp.float32)[:, None, None] * final_output
    ).astype(jnp.bfloat16)
    return (
        coupling_refreshed,
        sequence_refreshed.reshape(msa_rows, columns_here * features),
    )


def solution(mesh):
    placed = (P("row", "col", None), P("row", "col"), P(), P("row"), P(), P(), P(), P(), P())
    return jax.shard_map(
        shards,
        mesh=mesh,
        in_specs=placed,
        out_specs=(P("row", "col", None), P("row", "col")),
        check_vma=False,
    )
```

```python
import functools

import jax
import jax.numpy as jnp
import numpy as np
from jax import lax
from jax.experimental import pallas as pl
from jax.experimental.pallas import tpu as pltpu
from jax.sharding import PartitionSpec as P

epsilon = 1e-05
mask_offset = 1000000000.0
score_floor = -8192.0


def apply_layer_norm(array, along):
    average = jnp.mean(array, axis=along, keepdims=True)
    centred = array - average
    spread = jnp.mean(centred * centred, axis=along, keepdims=True)
    return centred * lax.rsqrt(spread + epsilon)


def exchange(blocks, axis):
    return lax.all_to_all(blocks, axis, split_axis=0, concat_axis=0, tiled=True)


def normed_rows(array):
    average = jnp.mean(array, axis=-1, keepdims=True)
    centred = array - average
    spread = jnp.mean(centred * centred, axis=-1, keepdims=True)
    return centred * lax.rsqrt(spread + epsilon)


def project_kernel(
    row_size, mask_far, pair_far, weight_far, sent, gate, mask, pair, weight, mixed, arrived
):
    copies = [
        pltpu.make_async_copy(pair_far, pair, arrived.at[0]),
        pltpu.make_async_copy(weight_far, weight, arrived.at[1]),
        pltpu.make_async_copy(mask_far, mask, arrived.at[2]),
    ]
    for copy in copies:
        copy.start()
    for copy in copies:
        copy.wait()
    rows, columns, channels = pair.shape
    patch = rows * columns
    here = channels // row_size
    normed = normed_rows(pair[...].astype(jnp.float32).reshape(patch, channels))
    normed = normed.astype(jnp.bfloat16)
    projected = lax.dot_general(
        weight[:, : 4 * channels],
        normed,
        (((0,), (1,)), ((), ())),
        preferred_element_type=jnp.float32,
    )
    lane = lax.broadcasted_iota(jnp.int32, (1, patch), 1)
    first_row = lax.axis_index("row") * rows
    first_column = lax.axis_index("col") * columns
    row_valid = jnp.zeros((1, patch), jnp.int32)
    column_valid = jnp.zeros((1, patch), jnp.int32)
    for i in range(rows):
        row_valid = jnp.where(lane // columns == i, mask[first_row + i], row_valid)
    for k in range(columns):
        column_valid = jnp.where(lane % columns == k, mask[first_column + k], column_valid)
    valid = (row_valid * column_valid).astype(jnp.float32)
    left = jax.nn.sigmoid(projected[:channels]) * projected[channels : 2 * channels] * valid
    right = (
        jax.nn.sigmoid(projected[2 * channels : 3 * channels])
        * projected[3 * channels : 4 * channels]
        * valid
    )
    for r in range(row_size):
        mixed[2 * r * here : (2 * r + 1) * here, :] = left[r * here : (r + 1) * here]
        mixed[(2 * r + 1) * here : (2 * r + 2) * here, :] = right[r * here : (r + 1) * here]
    sent[...] = mixed[...].astype(jnp.bfloat16)
    gate[...] = jax.nn.sigmoid(
        jnp.dot(normed, weight[:, 4 * channels :], preferred_element_type=jnp.float32)
    )


def tiled(rows, lanes):
    return lanes // min(lanes, 128), rows, min(lanes, 128)


def put_tiles(ref, value, rows=slice(None)):
    for tile in range(ref.shape[0]):
        ref[tile, rows, :] = value[:, tile * ref.shape[2] : (tile + 1) * ref.shape[2]]


def get_tiles(ref, rows):
    return jnp.concatenate([ref[tile, rows, :] for tile in range(ref.shape[0])], axis=1)


def regroup(pieces, here):
    lanes = pieces[0].shape[1]
    step = lanes // here
    group = lax.broadcasted_iota(jnp.int32, pieces[0].shape, 1) // step
    results = []
    for c in range(here):
        tiles = []
        for first in range(0, len(pieces), here):
            tile = pieces[first + c]
            for n in range(here):
                if n != c:
                    moved = pltpu.roll(pieces[first + n], (n - c) % here * step, axis=1)
                    tile = jnp.where(group == n, moved, tile)
            tiles.append(tile)
        results.append(jnp.concatenate(tiles, axis=1))
    return results


def gathered_kernel(columns, got, rider, sent, wide, turned):
    row_size, double, patch = got.shape
    here = double // 2
    rows = patch // columns
    put_tiles(wide, got[...].astype(jnp.float32).reshape(row_size * double, patch))
    sides = []
    for side in range(2):
        stacked = jnp.concatenate(
            [get_tiles(wide, pl.ds(side * here + c, row_size, stride=double)) for c in range(here)],
            axis=0,
        )
        turned[...] = stacked.T
        pieces = [turned[t * columns : (t + 1) * columns, :] for t in range(rows)]
        sides.append(
            [[block.astype(jnp.bfloat16) for block in regroup(pieces[h : h + rows // 2], here)]
             for h in (0, rows // 2)]
        )
    width = rows // 2 * row_size
    for c in range(here):
        for i in range(2):
            for j in range(2):
                place = (c * 2 + i) * 2 + j
                sent[place, :columns, :width] = sides[0][i][c]
                sent[place, :columns, width:] = sides[1][j][c]
                sent[place, columns:, :] = rider[place % 2]


def multiply_kernel(columns, row_size, got, crossed, wide):
    blocks = got.shape[0]
    width = got.shape[2] // 2
    both = jnp.concatenate([got[q, :columns, :] for q in range(blocks)], axis=0)
    product = lax.dot_general(
        both[:, width:], both[:, :width], (((0,), (0,)), ((), ())), preferred_element_type=jnp.float32
    )
    put_tiles(wide, product)
    half = width // row_size
    for q in range(blocks):
        crossed[q] = jnp.concatenate(
            [get_tiles(wide, pl.ds(2 * q + m, half, stride=row_size)) for m in range(2)], axis=0
        ).astype(jnp.bfloat16)


def returned_kernel(here, row_size, got, sent, wide):
    half = got.shape[1] // 2
    pieces = []
    for i in range(2):
        stacked = []
        for c in range(here):
            for m in range(2):
                for j in range(2):
                    place = (c * 2 + i) * 2 + j
                    stacked.append(got[place].astype(jnp.float32)[m * half : (m + 1) * half])
        turned = jnp.concatenate(stacked, axis=0).T
        pieces += [turned[t * row_size : (t + 1) * row_size] for t in range(half)]
    lanes = wide.shape[1]
    deep = wide.shape[0] // row_size
    for c, block in enumerate(regroup(pieces, here)):
        for tile in range(deep // here):
            wide[pl.ds(c * (deep // here) + tile, row_size, stride=deep), :] = block[
                :, tile * lanes : (tile + 1) * lanes
            ]
    sent[...] = wide[...].astype(jnp.bfloat16)


def update_kernel(
    columns, mask, all_valid, crossed, gate, pair, weight, bias, coupling, spread, wide
):
    patch, channels = pair.shape
    rows = patch // columns
    lanes = bias.shape[1]
    heads = lanes // rows
    wide[...] = crossed[...].astype(jnp.float32)
    tiles = crossed.shape[0] // channels
    cross = jnp.concatenate(
        [wide[pl.ds(tile, channels, stride=tiles), :] for tile in range(tiles)], axis=1
    )
    average = jnp.mean(cross, axis=0, keepdims=True)
    centred = cross - average
    variance = jnp.mean(centred * centred, axis=0, keepdims=True)
    cross = (centred * lax.rsqrt(variance + epsilon)).astype(jnp.bfloat16)
    update = lax.dot_general(
        cross, weight[...], (((0,), (0,)), ((), ())), preferred_element_type=jnp.float32
    )
    after = (pair[...].astype(jnp.float32) + gate[...] * update).astype(jnp.bfloat16)
    coupling[...] = after
    normed = normed_rows(after.astype(jnp.float32)).astype(jnp.bfloat16)
    lane = lax.broadcasted_iota(jnp.int32, (channels, lanes), 1)
    scores = jnp.zeros((columns, lanes), jnp.float32)
    for i in range(rows):
        own = jnp.where(lane // heads == i, bias[...], jnp.zeros((), jnp.bfloat16))
        scores = scores + jnp.dot(
            normed[i * columns : (i + 1) * columns], own, preferred_element_type=jnp.float32
        )
    place = lax.broadcasted_iota(jnp.int32, (columns, lanes), 0)
    first_column = lax.axis_index("col") * columns
    valid = jnp.zeros((columns, lanes), jnp.int32)
    for j in range(columns):
        valid = jnp.where(place == j, mask[first_column + j], valid)
    any_valid = jnp.max(all_valid[...], axis=1, keepdims=True)
    any_valid = jnp.max(any_valid, axis=0, keepdims=True) > 0
    scores = scores + (valid.astype(jnp.float32) - 1.0) * mask_offset
    scores = jnp.where(any_valid, jnp.maximum(scores, score_floor), scores + mask_offset)
    top = jnp.max(scores, axis=0, keepdims=True).astype(jnp.bfloat16).astype(jnp.float32)
    spread[:columns, :] = jnp.exp(scores - top)
    spread[columns:, :] = jnp.broadcast_to(top, (spread.shape[0] - columns, lanes))


def average(value_width, places, got, values, averaged, wide, ordered):
    blocks, deep, lanes = got.shape
    columns = deep - 8
    rows, across = averaged.shape
    heads = lanes // rows
    wide[...] = got[...].astype(jnp.float32)
    top = jnp.max(wide[:, columns : columns + 1, :], axis=0)
    total = jnp.zeros((1, lanes), jnp.float32)
    for block in range(blocks):
        place = places[block]
        factor = jnp.exp(wide[place, columns : columns + 1, :] - top)
        piece = wide[place, :columns, :] * factor
        total = total + jnp.sum(piece, axis=0, keepdims=True)
        ordered[block * columns : (block + 1) * columns, :] = piece
    weights = (ordered[...] / total).astype(jnp.bfloat16)
    own = lax.broadcasted_iota(jnp.int32, (lanes, value_width), 0) % heads == (
        lax.broadcasted_iota(jnp.int32, (lanes, value_width), 1) // (value_width // heads)
    )
    for start in range(0, across, value_width):
        product = lax.dot_general(
            weights,
            values[:, start : start + value_width],
            (((0,), (0,)), ((), ())),
            preferred_element_type=jnp.float32,
        )
        product = jnp.where(own, product, 0.0).reshape(rows, heads, value_width)
        averaged[:, start : start + value_width] = jnp.sum(product, axis=1)


def finish_kernel(
    value_width, features, places, flags, got, values, mine, gates, exits, tile, refreshed,
    other, wide, ordered, gated, lines,
):
    average(value_width, places, got, values, other, wide, ordered)
    half, across = mine.shape
    msa_rows = across // value_width
    low = lax.axis_index("row") < lax.axis_size("col")
    put_tiles(gated, gates[:half, :] * jnp.where(low, mine[...], other[...]), pl.ds(0, half))
    put_tiles(gated, gates[half:, :] * jnp.where(low, other[...], mine[...]), pl.ds(half, half))
    parts = gated.shape[0] // msa_rows
    for s in range(msa_rows):
        line = 0.0
        for parity in range(2):
            rows = jnp.concatenate(
                [gated[s * parts + part, pl.ds(parity, half, stride=2), :] for part in range(parts)],
                axis=1,
            ).astype(jnp.bfloat16)
            line = line + jnp.dot(rows, exits[parity], preferred_element_type=jnp.float32)
        lines[pl.ds(s, half, stride=msa_rows), :] = line
    place = lax.broadcasted_iota(jnp.int32, (msa_rows, 2 * features), 0)
    present = jnp.zeros((msa_rows, 2 * features), jnp.int32)
    for s in range(msa_rows):
        present = jnp.where(place == s, flags[s], present)
    present = present.astype(jnp.float32)
    for pair in range(half):
        lane = slice(pair * 2 * features, (pair + 1) * 2 * features)
        refreshed[:, lane] = (
            tile[:, lane].astype(jnp.float32)
            + present * lines[pair * msa_rows : (pair + 1) * msa_rows, :]
        ).astype(jnp.bfloat16)


def ring(a, b, size):
    return min((a - b) % size, (b - a) % size)


def score_places(row_size, col_size):
    around = col_size // 4
    offsets = sorted(range(-(col_size // 2) + 1, col_size // 2 + 1), key=abs)
    places = np.zeros((col_size, 2, col_size), np.int32)
    for row in range(row_size):
        to_col, to_x = row // 2, row % 2

        def far(col):
            x = ring(2 * (col // (col_size // 2)) + row // col_size,
                     2 * (to_col // (col_size // 2)) + to_x, 4)
            return x + ring(col // 2 % around, to_col // 2 % around, around) + (col ^ to_col) % 2

        order = sorted(range(col_size), key=far, reverse=True)
        for offset, col in zip(offsets, order):
            places[to_col, to_x, col] = (row + offset) % col_size
    return places


def shards(
    pair_state,
    sequence_embedding,
    token_valid_mask,
    sequence_present_flags,
    triangle_input_weight,
    triangle_output_weight,
    pair_head_bias,
    sequence_entry_matrix,
    sequence_exit_matrix,
):
    rows_here, columns_here, channels = pair_state.shape
    heads = pair_head_bias.shape[1]
    value_width = sequence_exit_matrix.shape[0]
    features = sequence_entry_matrix.shape[0]
    msa_rows = sequence_embedding.shape[0]
    row_index = lax.axis_index("row")
    col_index = lax.axis_index("col")
    row_size = lax.axis_size("row")
    col_size = lax.axis_size("col")
    fanout = row_size // col_size
    tokens = row_size * rows_here
    patch = rows_here * columns_here
    channels_here = channels // row_size
    width = tokens // 2
    lanes = min(patch, 128)
    places = score_places(row_size, col_size)
    moves = []
    for row in range(row_size):
        for col in range(col_size):
            to_row = row % fanout * col_size + int(places[row // fanout, row % fanout, col])
            moves.append((row * col_size + col, to_row * col_size + row // fanout))

    vmem = pl.BlockSpec(memory_space=pltpu.VMEM)
    smem = pl.BlockSpec(memory_space=pltpu.SMEM)
    spacious = pltpu.CompilerParams(vmem_limit_bytes=32 * 1024 * 1024)

    def work(flops):
        return pl.CostEstimate(flops=flops, bytes_accessed=2**20, transcendentals=0)

    sent, out_gate = pl.pallas_call(
        functools.partial(project_kernel, row_size),
        out_shape=(
            jax.ShapeDtypeStruct((2 * channels, patch), jnp.bfloat16),
            jax.ShapeDtypeStruct((patch, channels), jnp.float32),
        ),
        in_specs=[pl.BlockSpec(memory_space=pltpu.HBM)] * 3,
        out_specs=(vmem, vmem),
        scratch_shapes=[
            pltpu.SMEM(token_valid_mask.shape, jnp.int32),
            pltpu.VMEM(pair_state.shape, jnp.bfloat16),
            pltpu.VMEM(triangle_input_weight.shape, jnp.bfloat16),
            pltpu.VMEM((2 * channels, patch), jnp.float32),
            pltpu.SemaphoreType.DMA((3,)),
        ],
        compiler_params=pltpu.CompilerParams(vmem_limit_bytes=63 * 1024 * 1024),
        cost_estimate=work(10 * patch * channels * channels),
    )(token_valid_mask, pair_state, triangle_input_weight)

    got = exchange(sent.reshape(row_size, 2 * channels_here, patch), "row")
    rider = sequence_embedding.reshape(2, -1, 2 * width)
    sent = pl.pallas_call(
        functools.partial(gathered_kernel, columns_here),
        out_shape=jax.ShapeDtypeStruct(
            (col_size, columns_here + rider.shape[1], 2 * width), jnp.bfloat16
        ),
        in_specs=[vmem, vmem],
        out_specs=vmem,
        scratch_shapes=[
            pltpu.VMEM(tiled(2 * channels, patch), jnp.float32),
            pltpu.VMEM((patch, channels), jnp.float32),
        ],
        compiler_params=spacious,
        cost_estimate=work(patch * channels),
    )(got, rider)
    got = exchange(sent, "col")
    half = got[:, columns_here:]
    half_other = lax.ppermute(half, "col", [(a, a ^ 1) for a in range(col_size)])
    first = col_index % 2 == 0
    sequence_all = jnp.concatenate(
        [jnp.where(first, half, half_other), jnp.where(first, half_other, half)], axis=1
    ).reshape(col_size, msa_rows, columns_here, features)
    sent = pl.pallas_call(
        functools.partial(multiply_kernel, columns_here, row_size),
        out_shape=jax.ShapeDtypeStruct((col_size, rows_here, width), jnp.bfloat16),
        in_specs=[vmem],
        out_specs=vmem,
        scratch_shapes=[pltpu.VMEM(tiled(width, width), jnp.float32)],
        compiler_params=spacious,
        cost_estimate=work(2 * tokens * width * width),
    )(got)
    got = exchange(sent, "col")
    sent = pl.pallas_call(
        functools.partial(returned_kernel, channels_here, row_size),
        out_shape=jax.ShapeDtypeStruct((channels * patch // lanes, lanes), jnp.bfloat16),
        in_specs=[vmem],
        out_specs=vmem,
        scratch_shapes=[pltpu.VMEM((channels * patch // lanes, lanes), jnp.float32)],
        compiler_params=spacious,
        cost_estimate=work(patch * channels),
    )(got)
    crossed = exchange(sent.reshape(row_size, -1, lanes), "row").reshape(-1, lanes)
    coupling_refreshed, sent = pl.pallas_call(
        functools.partial(update_kernel, columns_here),
        out_shape=(
            jax.ShapeDtypeStruct((patch, channels), jnp.bfloat16),
            jax.ShapeDtypeStruct((columns_here + 8, rows_here * heads), jnp.float32),
        ),
        in_specs=[smem] + [vmem] * 6,
        out_specs=(vmem, vmem),
        scratch_shapes=[pltpu.VMEM((channels * patch // lanes, lanes), jnp.float32)],
        compiler_params=spacious,
        cost_estimate=work(4 * patch * channels * channels),
    )(
        token_valid_mask,
        token_valid_mask.reshape(4, -1),
        crossed,
        out_gate,
        pair_state.reshape(patch, channels),
        triangle_output_weight,
        jnp.tile(pair_head_bias, (1, rows_here)),
    )
    coupling_refreshed = coupling_refreshed.reshape(rows_here, columns_here, channels)
    sent = sent.astype(jnp.bfloat16)

    sent = lax.ppermute(sent, ("row", "col"), moves)
    groups = [[m * col_size + b for b in range(col_size)] for m in range(fanout)]
    mine = lax.all_to_all(
        jnp.broadcast_to(sent[None], (col_size,) + sent.shape),
        "row",
        split_axis=0,
        concat_axis=0,
        axis_index_groups=groups,
        tiled=True,
    )
    sequence_all = apply_layer_norm(sequence_all.astype(jnp.float32), 3).astype(jnp.bfloat16)
    values = jnp.einsum(
        "qsjf,fg->qjsg",
        sequence_all,
        sequence_entry_matrix[:, :value_width],
        preferred_element_type=jnp.float32,
    ).astype(jnp.bfloat16).reshape(tokens, msa_rows * value_width)
    places = lax.dynamic_index_in_dim(jnp.asarray(places), col_index, 0, keepdims=False)
    sequence_slab = sequence_embedding.reshape(msa_rows, columns_here, features).astype(jnp.float32)
    sequence_normed = apply_layer_norm(sequence_slab, 2).astype(jnp.bfloat16)
    sequence_switch = jax.nn.sigmoid(
        jnp.einsum(
            "sjf,fg->jsg",
            sequence_normed,
            sequence_entry_matrix[:, value_width:],
            preferred_element_type=jnp.float32,
        )
    ).reshape(columns_here, msa_rows * value_width)
    blank = jnp.zeros_like(sequence_exit_matrix)
    exits = jnp.stack(
        [
            jnp.concatenate([sequence_exit_matrix, blank], axis=1),
            jnp.concatenate([blank, sequence_exit_matrix], axis=1),
        ]
    )
    mine, values, sequence_switch, exits, places = lax.optimization_barrier(
        (mine, values, sequence_switch, exits, places)
    )
    swap = [(a, (a + col_size) % row_size) for a in range(row_size)]
    other = lax.ppermute(mine, "row", swap)

    half_index = row_index // col_size

    mine_places = lax.dynamic_index_in_dim(places, half_index, 0, keepdims=False)
    other_places = lax.dynamic_index_in_dim(places, 1 - half_index, 0, keepdims=False)
    across = msa_rows * value_width
    averaging = [
        pltpu.VMEM(mine.shape, jnp.float32),
        pltpu.VMEM((tokens, rows_here * heads), jnp.float32),
    ]
    flops = 2 * tokens * rows_here * heads * across
    mine = pl.pallas_call(
        functools.partial(average, value_width),
        out_shape=jax.ShapeDtypeStruct((rows_here, across), jnp.float32),
        in_specs=[smem, vmem, vmem],
        out_specs=vmem,
        scratch_shapes=averaging,
        compiler_params=spacious,
        cost_estimate=work(flops),
    )(mine_places, mine, values)
    sequence_refreshed = pl.pallas_call(
        functools.partial(finish_kernel, value_width, features),
        out_shape=jax.ShapeDtypeStruct(sequence_embedding.shape, jnp.bfloat16),
        in_specs=[smem, smem] + [vmem] * 6,
        out_specs=vmem,
        scratch_shapes=[pltpu.VMEM((rows_here, across), jnp.float32)]
        + averaging
        + [
            pltpu.VMEM(tiled(columns_here, across), jnp.float32),
            pltpu.VMEM((msa_rows * rows_here, 2 * features), jnp.float32),
        ],
        compiler_params=spacious,
        cost_estimate=work(flops),
    )(
        other_places,
        sequence_present_flags,
        other,
        values,
        mine,
        sequence_switch,
        exits,
        sequence_embedding,
    )
    return coupling_refreshed, sequence_refreshed


def solution(mesh):
    placed = (P("row", "col", None), P("row", "col"), P(), P("row"), P(), P(), P(), P(), P())
    return jax.shard_map(
        shards,
        mesh=mesh,
        in_specs=placed,
        out_specs=(P("row", "col", None), P("row", "col")),
        check_vma=False,
    )
```

```python
import functools

import jax
import jax.numpy as jnp
import numpy as np
from jax import lax
from jax.experimental import pallas as pl
from jax.experimental.pallas import tpu as pltpu
from jax.sharding import PartitionSpec as P

epsilon = 1e-05
mask_offset = 1000000000.0
score_floor = -8192.0


def apply_layer_norm(array, along):
    average = jnp.mean(array, axis=along, keepdims=True)
    centred = array - average
    spread = jnp.mean(centred * centred, axis=along, keepdims=True)
    return centred * lax.rsqrt(spread + epsilon)


def exchange(blocks, axis):
    return lax.all_to_all(blocks, axis, split_axis=0, concat_axis=0, tiled=True)


def normed_rows(array):
    average = jnp.mean(array, axis=-1, keepdims=True)
    centred = array - average
    spread = jnp.mean(centred * centred, axis=-1, keepdims=True)
    return centred * lax.rsqrt(spread + epsilon)


def project_kernel(
    row_size, mask_far, pair_far, weight_far, sent, gate, mask, pair, weight, mixed, arrived
):
    copies = [
        pltpu.make_async_copy(pair_far, pair, arrived.at[0]),
        pltpu.make_async_copy(weight_far, weight, arrived.at[1]),
        pltpu.make_async_copy(mask_far, mask, arrived.at[2]),
    ]
    for copy in copies:
        copy.start()
    for copy in copies:
        copy.wait()
    rows, columns, channels = pair.shape
    patch = rows * columns
    here = channels // row_size
    normed = normed_rows(pair[...].astype(jnp.float32).reshape(patch, channels))
    normed = normed.astype(jnp.bfloat16)
    projected = lax.dot_general(
        weight[:, : 4 * channels],
        normed,
        (((0,), (1,)), ((), ())),
        preferred_element_type=jnp.float32,
    )
    lane = lax.broadcasted_iota(jnp.int32, (1, patch), 1)
    first_row = lax.axis_index("row") * rows
    first_column = lax.axis_index("col") * columns
    row_valid = jnp.zeros((1, patch), jnp.int32)
    column_valid = jnp.zeros((1, patch), jnp.int32)
    for i in range(rows):
        row_valid = jnp.where(lane // columns == i, mask[first_row + i], row_valid)
    for k in range(columns):
        column_valid = jnp.where(lane % columns == k, mask[first_column + k], column_valid)
    valid = (row_valid * column_valid).astype(jnp.float32)
    left = jax.nn.sigmoid(projected[:channels]) * projected[channels : 2 * channels] * valid
    right = (
        jax.nn.sigmoid(projected[2 * channels : 3 * channels])
        * projected[3 * channels : 4 * channels]
        * valid
    )
    for r in range(row_size):
        mixed[2 * r * here : (2 * r + 1) * here, :] = left[r * here : (r + 1) * here]
        mixed[(2 * r + 1) * here : (2 * r + 2) * here, :] = right[r * here : (r + 1) * here]
    sent[...] = mixed[...].astype(jnp.bfloat16)
    gate[...] = jax.nn.sigmoid(
        jnp.dot(normed, weight[:, 4 * channels :], preferred_element_type=jnp.float32)
    )


def tiled(rows, lanes):
    return lanes // min(lanes, 128), rows, min(lanes, 128)


def put_tiles(ref, value, rows=slice(None)):
    for tile in range(ref.shape[0]):
        ref[tile, rows, :] = value[:, tile * ref.shape[2] : (tile + 1) * ref.shape[2]]


def get_tiles(ref, rows):
    return jnp.concatenate([ref[tile, rows, :] for tile in range(ref.shape[0])], axis=1)


def regroup(pieces, here):
    lanes = pieces[0].shape[1]
    step = lanes // here
    group = lax.broadcasted_iota(jnp.int32, pieces[0].shape, 1) // step
    results = []
    for c in range(here):
        tiles = []
        for first in range(0, len(pieces), here):
            tile = pieces[first + c]
            for n in range(here):
                if n != c:
                    moved = pltpu.roll(pieces[first + n], (n - c) % here * step, axis=1)
                    tile = jnp.where(group == n, moved, tile)
            tiles.append(tile)
        results.append(jnp.concatenate(tiles, axis=1))
    return results


def gathered_kernel(columns, got, rider, sent, wide, turned):
    row_size, double, patch = got.shape
    here = double // 2
    rows = patch // columns
    put_tiles(wide, got[...].astype(jnp.float32).reshape(row_size * double, patch))
    sides = []
    for side in range(2):
        stacked = jnp.concatenate(
            [get_tiles(wide, pl.ds(side * here + c, row_size, stride=double)) for c in range(here)],
            axis=0,
        )
        turned[...] = stacked.T
        pieces = [turned[t * columns : (t + 1) * columns, :] for t in range(rows)]
        sides.append(
            [[block.astype(jnp.bfloat16) for block in regroup(pieces[h : h + rows // 2], here)]
             for h in (0, rows // 2)]
        )
    width = rows // 2 * row_size
    for c in range(here):
        for i in range(2):
            for j in range(2):
                place = (c * 2 + i) * 2 + j
                sent[place, :columns, :width] = sides[0][i][c]
                sent[place, :columns, width:] = sides[1][j][c]
                sent[place, columns:, :] = rider[place % 4]


def multiply_kernel(columns, row_size, got, crossed, wide):
    blocks = got.shape[0]
    width = got.shape[2] // 2
    both = jnp.concatenate([got[q, :columns, :] for q in range(blocks)], axis=0)
    product = lax.dot_general(
        both[:, width:], both[:, :width], (((0,), (0,)), ((), ())), preferred_element_type=jnp.float32
    )
    put_tiles(wide, product)
    half = width // row_size
    for q in range(blocks):
        crossed[q] = jnp.concatenate(
            [get_tiles(wide, pl.ds(2 * q + m, half, stride=row_size)) for m in range(2)], axis=0
        ).astype(jnp.bfloat16)


def returned_kernel(here, row_size, got, sent, wide):
    half = got.shape[1] // 2
    pieces = []
    for i in range(2):
        stacked = []
        for c in range(here):
            for m in range(2):
                for j in range(2):
                    place = (c * 2 + i) * 2 + j
                    stacked.append(got[place].astype(jnp.float32)[m * half : (m + 1) * half])
        turned = jnp.concatenate(stacked, axis=0).T
        pieces += [turned[t * row_size : (t + 1) * row_size] for t in range(half)]
    lanes = wide.shape[1]
    deep = wide.shape[0] // row_size
    for c, block in enumerate(regroup(pieces, here)):
        for tile in range(deep // here):
            wide[pl.ds(c * (deep // here) + tile, row_size, stride=deep), :] = block[
                :, tile * lanes : (tile + 1) * lanes
            ]
    sent[...] = wide[...].astype(jnp.bfloat16)


def update_kernel(
    columns, mask, all_valid, crossed, gate, pair, weight, bias, coupling, spread, wide
):
    patch, channels = pair.shape
    rows = patch // columns
    lanes = bias.shape[1]
    heads = lanes // rows
    wide[...] = crossed[...].astype(jnp.float32)
    tiles = crossed.shape[0] // channels
    cross = jnp.concatenate(
        [wide[pl.ds(tile, channels, stride=tiles), :] for tile in range(tiles)], axis=1
    )
    average = jnp.mean(cross, axis=0, keepdims=True)
    centred = cross - average
    variance = jnp.mean(centred * centred, axis=0, keepdims=True)
    cross = (centred * lax.rsqrt(variance + epsilon)).astype(jnp.bfloat16)
    update = lax.dot_general(
        cross, weight[...], (((0,), (0,)), ((), ())), preferred_element_type=jnp.float32
    )
    after = (pair[...].astype(jnp.float32) + gate[...] * update).astype(jnp.bfloat16)
    coupling[...] = after
    normed = normed_rows(after.astype(jnp.float32)).astype(jnp.bfloat16)
    every = jnp.dot(normed, bias[...], preferred_element_type=jnp.float32)
    lane = lax.broadcasted_iota(jnp.int32, (columns, lanes), 1) // heads
    scores = jnp.zeros((columns, lanes), jnp.float32)
    for i in range(rows):
        scores = jnp.where(lane == i, every[i * columns : (i + 1) * columns], scores)
    place = lax.broadcasted_iota(jnp.int32, (columns, lanes), 0)
    first_column = lax.axis_index("col") * columns
    valid = jnp.zeros((columns, lanes), jnp.int32)
    for j in range(columns):
        valid = jnp.where(place == j, mask[first_column + j], valid)
    any_valid = jnp.max(all_valid[...], axis=1, keepdims=True)
    any_valid = jnp.max(any_valid, axis=0, keepdims=True) > 0
    scores = scores + (valid.astype(jnp.float32) - 1.0) * mask_offset
    scores = jnp.where(any_valid, jnp.maximum(scores, score_floor), scores + mask_offset)
    top = jnp.max(scores, axis=0, keepdims=True).astype(jnp.bfloat16).astype(jnp.float32)
    spread[:columns, :] = jnp.exp(scores - top)
    spread[columns:, :] = jnp.broadcast_to(top, (spread.shape[0] - columns, lanes))


def average(value_width, places, got, values, averaged, wide, ordered):
    blocks, deep, lanes = got.shape
    columns = deep - 8
    rows, across = averaged.shape
    heads = lanes // rows
    wide[...] = got[...].astype(jnp.float32)
    top = jnp.max(wide[:, columns : columns + 1, :], axis=0)
    total = jnp.zeros((1, lanes), jnp.float32)
    for block in range(blocks):
        place = places[block]
        factor = jnp.exp(wide[place, columns : columns + 1, :] - top)
        piece = wide[place, :columns, :] * factor
        total = total + jnp.sum(piece, axis=0, keepdims=True)
        ordered[block * columns : (block + 1) * columns, :] = piece
    weights = (ordered[...] / total).astype(jnp.bfloat16)
    own = lax.broadcasted_iota(jnp.int32, (lanes, value_width), 0) % heads == (
        lax.broadcasted_iota(jnp.int32, (lanes, value_width), 1) // (value_width // heads)
    )
    for start in range(0, across, value_width):
        product = lax.dot_general(
            weights,
            values[:, start : start + value_width],
            (((0,), (0,)), ((), ())),
            preferred_element_type=jnp.float32,
        )
        product = jnp.where(own, product, 0.0).reshape(rows, heads, value_width)
        averaged[:, start : start + value_width] = jnp.sum(product, axis=1)


def finish_kernel(
    value_width, features, places, flags, got, values, mine, gates, exits, tile, refreshed,
    other, wide, ordered, gated, lines,
):
    average(value_width, places, got, values, other, wide, ordered)
    half, across = mine.shape
    msa_rows = across // value_width
    low = lax.axis_index("row") < lax.axis_size("col")
    put_tiles(gated, gates[:half, :] * jnp.where(low, mine[...], other[...]), pl.ds(0, half))
    put_tiles(gated, gates[half:, :] * jnp.where(low, other[...], mine[...]), pl.ds(half, half))
    parts = gated.shape[0] // msa_rows
    for s in range(msa_rows):
        line = 0.0
        for parity in range(2):
            rows = jnp.concatenate(
                [gated[s * parts + part, pl.ds(parity, half, stride=2), :] for part in range(parts)],
                axis=1,
            ).astype(jnp.bfloat16)
            line = line + jnp.dot(rows, exits[parity], preferred_element_type=jnp.float32)
        lines[pl.ds(s, half, stride=msa_rows), :] = line
    place = lax.broadcasted_iota(jnp.int32, (msa_rows, 2 * features), 0)
    present = jnp.zeros((msa_rows, 2 * features), jnp.int32)
    for s in range(msa_rows):
        present = jnp.where(place == s, flags[s], present)
    present = present.astype(jnp.float32)
    for pair in range(half):
        lane = slice(pair * 2 * features, (pair + 1) * 2 * features)
        refreshed[:, lane] = (
            tile[:, lane].astype(jnp.float32)
            + present * lines[pair * msa_rows : (pair + 1) * msa_rows, :]
        ).astype(jnp.bfloat16)


def ring(a, b, size):
    return min((a - b) % size, (b - a) % size)


def score_places(row_size, col_size):
    around = col_size // 4
    offsets = sorted(range(-(col_size // 2) + 1, col_size // 2 + 1), key=abs)
    places = np.zeros((col_size, 2, col_size), np.int32)
    for row in range(row_size):
        to_col, to_x = row // 2, row % 2

        def far(col):
            x = ring(2 * (col // (col_size // 2)) + row // col_size,
                     2 * (to_col // (col_size // 2)) + to_x, 4)
            return x + ring(col // 2 % around, to_col // 2 % around, around) + (col ^ to_col) % 2

        order = sorted(range(col_size), key=far, reverse=True)
        for offset, col in zip(offsets, order):
            places[to_col, to_x, col] = (row + offset) % col_size
    return places


def shards(
    pair_state,
    sequence_embedding,
    token_valid_mask,
    sequence_present_flags,
    triangle_input_weight,
    triangle_output_weight,
    pair_head_bias,
    sequence_entry_matrix,
    sequence_exit_matrix,
):
    rows_here, columns_here, channels = pair_state.shape
    heads = pair_head_bias.shape[1]
    value_width = sequence_exit_matrix.shape[0]
    features = sequence_entry_matrix.shape[0]
    msa_rows = sequence_embedding.shape[0]
    row_index = lax.axis_index("row")
    col_index = lax.axis_index("col")
    row_size = lax.axis_size("row")
    col_size = lax.axis_size("col")
    fanout = row_size // col_size
    tokens = row_size * rows_here
    patch = rows_here * columns_here
    channels_here = channels // row_size
    width = tokens // 2
    lanes = min(patch, 128)
    places = score_places(row_size, col_size)
    moves = []
    for row in range(row_size):
        for col in range(col_size):
            to_row = row % fanout * col_size + int(places[row // fanout, row % fanout, col])
            moves.append((row * col_size + col, to_row * col_size + row // fanout))

    vmem = pl.BlockSpec(memory_space=pltpu.VMEM)
    smem = pl.BlockSpec(memory_space=pltpu.SMEM)
    spacious = pltpu.CompilerParams(vmem_limit_bytes=32 * 1024 * 1024)

    def work(flops):
        return pl.CostEstimate(flops=flops, bytes_accessed=2**20, transcendentals=0)

    sent, out_gate = pl.pallas_call(
        functools.partial(project_kernel, row_size),
        out_shape=(
            jax.ShapeDtypeStruct((2 * channels, patch), jnp.bfloat16),
            jax.ShapeDtypeStruct((patch, channels), jnp.float32),
        ),
        in_specs=[pl.BlockSpec(memory_space=pltpu.HBM)] * 3,
        out_specs=(vmem, vmem),
        scratch_shapes=[
            pltpu.SMEM(token_valid_mask.shape, jnp.int32),
            pltpu.VMEM(pair_state.shape, jnp.bfloat16),
            pltpu.VMEM(triangle_input_weight.shape, jnp.bfloat16),
            pltpu.VMEM((2 * channels, patch), jnp.float32),
            pltpu.SemaphoreType.DMA((3,)),
        ],
        compiler_params=pltpu.CompilerParams(vmem_limit_bytes=63 * 1024 * 1024),
        cost_estimate=work(10 * patch * channels * channels),
    )(token_valid_mask, pair_state, triangle_input_weight)

    got = exchange(sent.reshape(row_size, 2 * channels_here, patch), "row")
    rider = sequence_embedding.reshape(4, -1, 2 * width)
    sent = pl.pallas_call(
        functools.partial(gathered_kernel, columns_here),
        out_shape=jax.ShapeDtypeStruct(
            (col_size, columns_here + rider.shape[1], 2 * width), jnp.bfloat16
        ),
        in_specs=[vmem, vmem],
        out_specs=vmem,
        scratch_shapes=[
            pltpu.VMEM(tiled(2 * channels, patch), jnp.float32),
            pltpu.VMEM((patch, channels), jnp.float32),
        ],
        compiler_params=spacious,
        cost_estimate=work(patch * channels),
    )(got, rider)
    got = exchange(sent, "col")
    share = got[:, columns_here:]
    for step in (1, 2):
        swapped = lax.ppermute(share, "col", [(a, a ^ step) for a in range(col_size)])
        first = col_index // step % 2 == 0
        share = jnp.concatenate(
            [jnp.where(first, share, swapped), jnp.where(first, swapped, share)], axis=1
        )
    sequence_all = share.reshape(col_size, msa_rows, columns_here, features)
    sent = pl.pallas_call(
        functools.partial(multiply_kernel, columns_here, row_size),
        out_shape=jax.ShapeDtypeStruct((col_size, rows_here, width), jnp.bfloat16),
        in_specs=[vmem],
        out_specs=vmem,
        scratch_shapes=[pltpu.VMEM(tiled(width, width), jnp.float32)],
        compiler_params=spacious,
        cost_estimate=work(2 * tokens * width * width),
    )(got)
    got = exchange(sent, "col")
    sent = pl.pallas_call(
        functools.partial(returned_kernel, channels_here, row_size),
        out_shape=jax.ShapeDtypeStruct((channels * patch // lanes, lanes), jnp.bfloat16),
        in_specs=[vmem],
        out_specs=vmem,
        scratch_shapes=[pltpu.VMEM((channels * patch // lanes, lanes), jnp.float32)],
        compiler_params=spacious,
        cost_estimate=work(patch * channels),
    )(got)
    crossed = exchange(sent.reshape(row_size, -1, lanes), "row").reshape(-1, lanes)
    coupling_refreshed, sent = pl.pallas_call(
        functools.partial(update_kernel, columns_here),
        out_shape=(
            jax.ShapeDtypeStruct((patch, channels), jnp.bfloat16),
            jax.ShapeDtypeStruct((columns_here + 8, rows_here * heads), jnp.float32),
        ),
        in_specs=[smem] + [vmem] * 6,
        out_specs=(vmem, vmem),
        scratch_shapes=[pltpu.VMEM((channels * patch // lanes, lanes), jnp.float32)],
        compiler_params=spacious,
        cost_estimate=work(4 * patch * channels * channels),
    )(
        token_valid_mask,
        token_valid_mask.reshape(4, -1),
        crossed,
        out_gate,
        pair_state.reshape(patch, channels),
        triangle_output_weight,
        jnp.tile(pair_head_bias, (1, rows_here)),
    )
    coupling_refreshed = coupling_refreshed.reshape(rows_here, columns_here, channels)
    sent = sent.astype(jnp.bfloat16)

    sent = lax.ppermute(sent, ("row", "col"), moves)
    groups = [[m * col_size + b for b in range(col_size)] for m in range(fanout)]
    mine = lax.all_to_all(
        jnp.broadcast_to(sent[None], (col_size,) + sent.shape),
        "row",
        split_axis=0,
        concat_axis=0,
        axis_index_groups=groups,
        tiled=True,
    )
    sequence_all = apply_layer_norm(sequence_all.astype(jnp.float32), 3).astype(jnp.bfloat16)
    values = jnp.einsum(
        "qsjf,fg->qjsg",
        sequence_all,
        sequence_entry_matrix[:, :value_width],
        preferred_element_type=jnp.float32,
    ).astype(jnp.bfloat16).reshape(tokens, msa_rows * value_width)
    places = lax.dynamic_index_in_dim(jnp.asarray(places), col_index, 0, keepdims=False)
    sequence_slab = sequence_embedding.reshape(msa_rows, columns_here, features).astype(jnp.float32)
    sequence_normed = apply_layer_norm(sequence_slab, 2).astype(jnp.bfloat16)
    sequence_switch = jax.nn.sigmoid(
        jnp.einsum(
            "sjf,fg->jsg",
            sequence_normed,
            sequence_entry_matrix[:, value_width:],
            preferred_element_type=jnp.float32,
        )
    ).reshape(columns_here, msa_rows * value_width)
    blank = jnp.zeros_like(sequence_exit_matrix)
    exits = jnp.stack(
        [
            jnp.concatenate([sequence_exit_matrix, blank], axis=1),
            jnp.concatenate([blank, sequence_exit_matrix], axis=1),
        ]
    )
    mine, values, sequence_switch, exits, places = lax.optimization_barrier(
        (mine, values, sequence_switch, exits, places)
    )
    swap = [(a, (a + col_size) % row_size) for a in range(row_size)]
    other = lax.ppermute(mine, "row", swap)

    half_index = row_index // col_size

    mine_places = lax.dynamic_index_in_dim(places, half_index, 0, keepdims=False)
    other_places = lax.dynamic_index_in_dim(places, 1 - half_index, 0, keepdims=False)
    across = msa_rows * value_width
    averaging = [
        pltpu.VMEM(mine.shape, jnp.float32),
        pltpu.VMEM((tokens, rows_here * heads), jnp.float32),
    ]
    flops = 2 * tokens * rows_here * heads * across
    mine = pl.pallas_call(
        functools.partial(average, value_width),
        out_shape=jax.ShapeDtypeStruct((rows_here, across), jnp.float32),
        in_specs=[smem, vmem, vmem],
        out_specs=vmem,
        scratch_shapes=averaging,
        compiler_params=spacious,
        cost_estimate=work(flops),
    )(mine_places, mine, values)
    sequence_refreshed = pl.pallas_call(
        functools.partial(finish_kernel, value_width, features),
        out_shape=jax.ShapeDtypeStruct(sequence_embedding.shape, jnp.bfloat16),
        in_specs=[smem, smem] + [vmem] * 6,
        out_specs=vmem,
        scratch_shapes=[pltpu.VMEM((rows_here, across), jnp.float32)]
        + averaging
        + [
            pltpu.VMEM(tiled(columns_here, across), jnp.float32),
            pltpu.VMEM((msa_rows * rows_here, 2 * features), jnp.float32),
        ],
        compiler_params=spacious,
        cost_estimate=work(flops),
    )(
        other_places,
        sequence_present_flags,
        other,
        values,
        mine,
        sequence_switch,
        exits,
        sequence_embedding,
    )
    return coupling_refreshed, sequence_refreshed


def solution(mesh):
    placed = (P("row", "col", None), P("row", "col"), P(), P("row"), P(), P(), P(), P(), P())
    return jax.shard_map(
        shards,
        mesh=mesh,
        in_specs=placed,
        out_specs=(P("row", "col", None), P("row", "col")),
        check_vma=False,
    )
```

```python
import functools

import jax
import jax.numpy as jnp
import numpy as np
from jax import lax
from jax.experimental import pallas as pl
from jax.experimental.pallas import tpu as pltpu
from jax.sharding import PartitionSpec as P

epsilon = 1e-05
mask_offset = 1000000000.0
score_floor = -8192.0


def apply_layer_norm(array, along):
    average = jnp.mean(array, axis=along, keepdims=True)
    centred = array - average
    spread = jnp.mean(centred * centred, axis=along, keepdims=True)
    return centred * lax.rsqrt(spread + epsilon)


def exchange(blocks, axis):
    return lax.all_to_all(blocks, axis, split_axis=0, concat_axis=0, tiled=True)


def normed_rows(array):
    average = jnp.mean(array, axis=-1, keepdims=True)
    centred = array - average
    spread = jnp.mean(centred * centred, axis=-1, keepdims=True)
    return centred * lax.rsqrt(spread + epsilon)


def project_kernel(
    row_size, mask_far, pair_far, weight_far, sent, gate, mask, pair, weight, mixed, arrived
):
    copies = [
        pltpu.make_async_copy(pair_far, pair, arrived.at[0]),
        pltpu.make_async_copy(weight_far, weight, arrived.at[1]),
        pltpu.make_async_copy(mask_far, mask, arrived.at[2]),
    ]
    for copy in copies:
        copy.start()
    for copy in copies:
        copy.wait()
    rows, columns, channels = pair.shape
    patch = rows * columns
    here = channels // row_size
    normed = normed_rows(pair[...].astype(jnp.float32).reshape(patch, channels))
    normed = normed.astype(jnp.bfloat16)
    projected = lax.dot_general(
        weight[:, : 4 * channels],
        normed,
        (((0,), (1,)), ((), ())),
        preferred_element_type=jnp.float32,
    )
    lane = lax.broadcasted_iota(jnp.int32, (1, patch), 1)
    first_row = lax.axis_index("row") * rows
    first_column = lax.axis_index("col") * columns
    row_valid = jnp.zeros((1, patch), jnp.int32)
    column_valid = jnp.zeros((1, patch), jnp.int32)
    for i in range(rows):
        row_valid = jnp.where(lane // columns == i, mask[first_row + i], row_valid)
    for k in range(columns):
        column_valid = jnp.where(lane % columns == k, mask[first_column + k], column_valid)
    valid = (row_valid * column_valid).astype(jnp.float32)
    left = jax.nn.sigmoid(projected[:channels]) * projected[channels : 2 * channels] * valid
    right = (
        jax.nn.sigmoid(projected[2 * channels : 3 * channels])
        * projected[3 * channels : 4 * channels]
        * valid
    )
    for r in range(row_size):
        mixed[2 * r * here : (2 * r + 1) * here, :] = left[r * here : (r + 1) * here]
        mixed[(2 * r + 1) * here : (2 * r + 2) * here, :] = right[r * here : (r + 1) * here]
    sent[...] = mixed[...].astype(jnp.bfloat16)
    gate[...] = jax.nn.sigmoid(
        jnp.dot(normed, weight[:, 4 * channels :], preferred_element_type=jnp.float32)
    )


def tiled(rows, lanes):
    return lanes // min(lanes, 128), rows, min(lanes, 128)


def put_tiles(ref, value, rows=slice(None)):
    for tile in range(ref.shape[0]):
        ref[tile, rows, :] = value[:, tile * ref.shape[2] : (tile + 1) * ref.shape[2]]


def get_tiles(ref, rows):
    return jnp.concatenate([ref[tile, rows, :] for tile in range(ref.shape[0])], axis=1)


def regroup(pieces, here):
    lanes = pieces[0].shape[1]
    step = lanes // here
    group = lax.broadcasted_iota(jnp.int32, pieces[0].shape, 1) // step
    results = []
    for c in range(here):
        tiles = []
        for first in range(0, len(pieces), here):
            tile = pieces[first + c]
            for n in range(here):
                if n != c:
                    moved = pltpu.roll(pieces[first + n], (n - c) % here * step, axis=1)
                    tile = jnp.where(group == n, moved, tile)
            tiles.append(tile)
        results.append(jnp.concatenate(tiles, axis=1))
    return results


def gathered_kernel(columns, got, rider, sent, wide, turned):
    row_size, double, patch = got.shape
    here = double // 2
    rows = patch // columns
    put_tiles(wide, got[...].astype(jnp.float32).reshape(row_size * double, patch))
    sides = []
    for side in range(2):
        stacked = jnp.concatenate(
            [get_tiles(wide, pl.ds(side * here + c, row_size, stride=double)) for c in range(here)],
            axis=0,
        )
        turned[...] = stacked.T
        pieces = [turned[t * columns : (t + 1) * columns, :] for t in range(rows)]
        sides.append(
            [[block.astype(jnp.bfloat16) for block in regroup(pieces[h : h + rows // 2], here)]
             for h in (0, rows // 2)]
        )
    width = rows // 2 * row_size
    for c in range(here):
        for i in range(2):
            for j in range(2):
                place = (c * 2 + i) * 2 + j
                sent[place, :columns, :width] = sides[0][i][c]
                sent[place, :columns, width:] = sides[1][j][c]
                sent[place, columns:, :] = rider[place % 4]


def multiply_kernel(columns, row_size, got, crossed, wide):
    blocks = got.shape[0]
    width = got.shape[2] // 2
    both = jnp.concatenate([got[q, :columns, :] for q in range(blocks)], axis=0)
    product = lax.dot_general(
        both[:, width:], both[:, :width], (((0,), (0,)), ((), ())), preferred_element_type=jnp.float32
    )
    put_tiles(wide, product)
    half = width // row_size
    for q in range(blocks):
        crossed[q] = jnp.concatenate(
            [get_tiles(wide, pl.ds(2 * q + m, half, stride=row_size)) for m in range(2)], axis=0
        ).astype(jnp.bfloat16)


def returned_kernel(here, row_size, got, sent, wide):
    half = got.shape[1] // 2
    pieces = []
    for i in range(2):
        stacked = []
        for c in range(here):
            for m in range(2):
                for j in range(2):
                    place = (c * 2 + i) * 2 + j
                    stacked.append(got[place].astype(jnp.float32)[m * half : (m + 1) * half])
        turned = jnp.concatenate(stacked, axis=0).T
        pieces += [turned[t * row_size : (t + 1) * row_size] for t in range(half)]
    lanes = wide.shape[1]
    deep = wide.shape[0] // row_size
    for c, block in enumerate(regroup(pieces, here)):
        for tile in range(deep // here):
            wide[pl.ds(c * (deep // here) + tile, row_size, stride=deep), :] = block[
                :, tile * lanes : (tile + 1) * lanes
            ]
    sent[...] = wide[...].astype(jnp.bfloat16)


def update_kernel(
    columns, mask, all_valid, crossed, gate, pair, weight, bias, coupling, spread, wide
):
    patch, channels = pair.shape
    rows = patch // columns
    lanes = bias.shape[1]
    heads = lanes // rows
    wide[...] = crossed[...].astype(jnp.float32)
    tiles = crossed.shape[0] // channels
    cross = jnp.concatenate(
        [wide[pl.ds(tile, channels, stride=tiles), :] for tile in range(tiles)], axis=1
    )
    average = jnp.mean(cross, axis=0, keepdims=True)
    centred = cross - average
    variance = jnp.mean(centred * centred, axis=0, keepdims=True)
    cross = (centred * lax.rsqrt(variance + epsilon)).astype(jnp.bfloat16)
    update = lax.dot_general(
        cross, weight[...], (((0,), (0,)), ((), ())), preferred_element_type=jnp.float32
    )
    after = (pair[...].astype(jnp.float32) + gate[...] * update).astype(jnp.bfloat16)
    coupling[...] = after
    normed = normed_rows(after.astype(jnp.float32)).astype(jnp.bfloat16)
    every = jnp.dot(normed, bias[...], preferred_element_type=jnp.float32)
    lane = lax.broadcasted_iota(jnp.int32, (columns, lanes), 1) // heads
    scores = jnp.zeros((columns, lanes), jnp.float32)
    for i in range(rows):
        scores = jnp.where(lane == i, every[i * columns : (i + 1) * columns], scores)
    place = lax.broadcasted_iota(jnp.int32, (columns, lanes), 0)
    first_column = lax.axis_index("col") * columns
    valid = jnp.zeros((columns, lanes), jnp.int32)
    for j in range(columns):
        valid = jnp.where(place == j, mask[first_column + j], valid)
    any_valid = jnp.max(all_valid[...], axis=1, keepdims=True)
    any_valid = jnp.max(any_valid, axis=0, keepdims=True) > 0
    scores = scores + (valid.astype(jnp.float32) - 1.0) * mask_offset
    scores = jnp.where(any_valid, jnp.maximum(scores, score_floor), scores + mask_offset)
    top = jnp.max(scores, axis=0, keepdims=True).astype(jnp.bfloat16).astype(jnp.float32)
    spread[:columns, :] = jnp.exp(scores - top)
    spread[columns:, :] = jnp.broadcast_to(top, (spread.shape[0] - columns, lanes))


def average(value_width, places, got, values, averaged, wide, ordered):
    blocks, deep, lanes = got.shape
    columns = deep - 8
    rows, across = averaged.shape
    heads = lanes // rows
    wide[...] = got[...].astype(jnp.float32)
    top = jnp.max(wide[:, columns : columns + 1, :], axis=0)
    total = jnp.zeros((1, lanes), jnp.float32)
    for block in range(blocks):
        place = places[block]
        factor = jnp.exp(wide[place, columns : columns + 1, :] - top)
        piece = wide[place, :columns, :] * factor
        total = total + jnp.sum(piece, axis=0, keepdims=True)
        ordered[block * columns : (block + 1) * columns, :] = piece
    weights = (ordered[...] / total).astype(jnp.bfloat16)
    own = lax.broadcasted_iota(jnp.int32, (lanes, value_width), 0) % heads == (
        lax.broadcasted_iota(jnp.int32, (lanes, value_width), 1) // (value_width // heads)
    )
    for start in range(0, across, value_width):
        product = lax.dot_general(
            weights,
            values[:, start : start + value_width],
            (((0,), (0,)), ((), ())),
            preferred_element_type=jnp.float32,
        )
        product = jnp.where(own, product, 0.0).reshape(rows, heads, value_width)
        averaged[:, start : start + value_width] = jnp.sum(product, axis=1)


def finish_kernel(
    value_width, features, places, flags, got, values, mine, gates, exits, tile, refreshed,
    other, wide, ordered, gated, lines,
):
    average(value_width, places, got, values, other, wide, ordered)
    half, across = mine.shape
    msa_rows = across // value_width
    low = lax.axis_index("row") < lax.axis_size("col")
    put_tiles(gated, gates[:half, :] * jnp.where(low, mine[...], other[...]), pl.ds(0, half))
    put_tiles(gated, gates[half:, :] * jnp.where(low, other[...], mine[...]), pl.ds(half, half))
    parts = gated.shape[0] // msa_rows
    for s in range(msa_rows):
        line = 0.0
        for parity in range(2):
            rows = jnp.concatenate(
                [gated[s * parts + part, pl.ds(parity, half, stride=2), :] for part in range(parts)],
                axis=1,
            ).astype(jnp.bfloat16)
            line = line + jnp.dot(rows, exits[parity], preferred_element_type=jnp.float32)
        lines[pl.ds(s, half, stride=msa_rows), :] = line
    place = lax.broadcasted_iota(jnp.int32, (msa_rows, 2 * features), 0)
    present = jnp.zeros((msa_rows, 2 * features), jnp.int32)
    for s in range(msa_rows):
        present = jnp.where(place == s, flags[s], present)
    present = present.astype(jnp.float32)
    for pair in range(half):
        lane = slice(pair * 2 * features, (pair + 1) * 2 * features)
        refreshed[:, lane] = (
            tile[:, lane].astype(jnp.float32)
            + present * lines[pair * msa_rows : (pair + 1) * msa_rows, :]
        ).astype(jnp.bfloat16)


def ring(a, b, size):
    return min((a - b) % size, (b - a) % size)


def score_places(row_size, col_size):
    around = col_size // 4
    offsets = sorted(range(-(col_size // 2) + 1, col_size // 2 + 1), key=abs)
    places = np.zeros((col_size, 2, col_size), np.int32)
    for row in range(row_size):
        to_col, to_x = row // 2, row % 2

        def far(col):
            x = ring(2 * (col // (col_size // 2)) + row // col_size,
                     2 * (to_col // (col_size // 2)) + to_x, 4)
            return x + ring(col // 2 % around, to_col // 2 % around, around) + (col ^ to_col) % 2

        order = sorted(range(col_size), key=far, reverse=True)
        for offset, col in zip(offsets, order):
            places[to_col, to_x, col] = (row + offset) % col_size
    return places


def shards(
    pair_state,
    sequence_embedding,
    token_valid_mask,
    sequence_present_flags,
    triangle_input_weight,
    triangle_output_weight,
    pair_head_bias,
    sequence_entry_matrix,
    sequence_exit_matrix,
):
    rows_here, columns_here, channels = pair_state.shape
    heads = pair_head_bias.shape[1]
    value_width = sequence_exit_matrix.shape[0]
    features = sequence_entry_matrix.shape[0]
    msa_rows = sequence_embedding.shape[0]
    row_index = lax.axis_index("row")
    col_index = lax.axis_index("col")
    row_size = lax.axis_size("row")
    col_size = lax.axis_size("col")
    fanout = row_size // col_size
    tokens = row_size * rows_here
    patch = rows_here * columns_here
    channels_here = channels // row_size
    width = tokens // 2
    lanes = min(patch, 128)
    places = score_places(row_size, col_size)
    moves = []
    for row in range(row_size):
        for col in range(col_size):
            to_row = row % fanout * col_size + int(places[row // fanout, row % fanout, col])
            moves.append((row * col_size + col, to_row * col_size + row // fanout))

    vmem = pl.BlockSpec(memory_space=pltpu.VMEM)
    smem = pl.BlockSpec(memory_space=pltpu.SMEM)
    spacious = pltpu.CompilerParams(vmem_limit_bytes=32 * 1024 * 1024)

    def work(flops):
        return pl.CostEstimate(flops=flops, bytes_accessed=2**20, transcendentals=0)

    sent, out_gate = pl.pallas_call(
        functools.partial(project_kernel, row_size),
        out_shape=(
            jax.ShapeDtypeStruct((2 * channels, patch), jnp.bfloat16),
            jax.ShapeDtypeStruct((patch, channels), jnp.float32),
        ),
        in_specs=[pl.BlockSpec(memory_space=pltpu.HBM)] * 3,
        out_specs=(vmem, vmem),
        scratch_shapes=[
            pltpu.SMEM(token_valid_mask.shape, jnp.int32),
            pltpu.VMEM(pair_state.shape, jnp.bfloat16),
            pltpu.VMEM(triangle_input_weight.shape, jnp.bfloat16),
            pltpu.VMEM((2 * channels, patch), jnp.float32),
            pltpu.SemaphoreType.DMA((3,)),
        ],
        compiler_params=pltpu.CompilerParams(vmem_limit_bytes=63 * 1024 * 1024),
        cost_estimate=work(10 * patch * channels * channels),
    )(token_valid_mask, pair_state, triangle_input_weight)

    got = exchange(sent.reshape(row_size, 2 * channels_here, patch), "row")
    rider = sequence_embedding.reshape(4, -1, 2 * width)
    sent = pl.pallas_call(
        functools.partial(gathered_kernel, columns_here),
        out_shape=jax.ShapeDtypeStruct(
            (col_size, columns_here + rider.shape[1], 2 * width), jnp.bfloat16
        ),
        in_specs=[vmem, vmem],
        out_specs=vmem,
        scratch_shapes=[
            pltpu.VMEM(tiled(2 * channels, patch), jnp.float32),
            pltpu.VMEM((patch, channels), jnp.float32),
        ],
        compiler_params=spacious,
        cost_estimate=work(patch * channels),
    )(got, rider)
    got = exchange(sent, "col")
    share = got[:, columns_here:]

    def swap_share(share, step):
        swapped = lax.ppermute(share, "col", [(a, a ^ step) for a in range(col_size)])
        first = col_index // step % 2 == 0
        return jnp.concatenate(
            [jnp.where(first, share, swapped), jnp.where(first, swapped, share)], axis=1
        )

    sent = pl.pallas_call(
        functools.partial(multiply_kernel, columns_here, row_size),
        out_shape=jax.ShapeDtypeStruct((col_size, rows_here, width), jnp.bfloat16),
        in_specs=[vmem],
        out_specs=vmem,
        scratch_shapes=[pltpu.VMEM(tiled(width, width), jnp.float32)],
        compiler_params=spacious,
        cost_estimate=work(2 * tokens * width * width),
    )(got)
    share, sent = lax.optimization_barrier((share, sent))
    share = swap_share(share, 1)
    got = exchange(sent, "col")
    sent = pl.pallas_call(
        functools.partial(returned_kernel, channels_here, row_size),
        out_shape=jax.ShapeDtypeStruct((channels * patch // lanes, lanes), jnp.bfloat16),
        in_specs=[vmem],
        out_specs=vmem,
        scratch_shapes=[pltpu.VMEM((channels * patch // lanes, lanes), jnp.float32)],
        compiler_params=spacious,
        cost_estimate=work(patch * channels),
    )(got)
    share, sent = lax.optimization_barrier((share, sent))
    sequence_all = swap_share(share, 2).reshape(col_size, msa_rows, columns_here, features)
    crossed = exchange(sent.reshape(row_size, -1, lanes), "row").reshape(-1, lanes)
    coupling_refreshed, sent = pl.pallas_call(
        functools.partial(update_kernel, columns_here),
        out_shape=(
            jax.ShapeDtypeStruct((patch, channels), jnp.bfloat16),
            jax.ShapeDtypeStruct((columns_here + 8, rows_here * heads), jnp.float32),
        ),
        in_specs=[smem] + [vmem] * 6,
        out_specs=(vmem, vmem),
        scratch_shapes=[pltpu.VMEM((channels * patch // lanes, lanes), jnp.float32)],
        compiler_params=spacious,
        cost_estimate=work(4 * patch * channels * channels),
    )(
        token_valid_mask,
        token_valid_mask.reshape(4, -1),
        crossed,
        out_gate,
        pair_state.reshape(patch, channels),
        triangle_output_weight,
        jnp.tile(pair_head_bias, (1, rows_here)),
    )
    coupling_refreshed = coupling_refreshed.reshape(rows_here, columns_here, channels)
    sent = sent.astype(jnp.bfloat16)

    sent = lax.ppermute(sent, ("row", "col"), moves)
    groups = [[m * col_size + b for b in range(col_size)] for m in range(fanout)]
    mine = lax.all_to_all(
        jnp.broadcast_to(sent[None], (col_size,) + sent.shape),
        "row",
        split_axis=0,
        concat_axis=0,
        axis_index_groups=groups,
        tiled=True,
    )
    sequence_all = apply_layer_norm(sequence_all.astype(jnp.float32), 3).astype(jnp.bfloat16)
    values = jnp.einsum(
        "qsjf,fg->qjsg",
        sequence_all,
        sequence_entry_matrix[:, :value_width],
        preferred_element_type=jnp.float32,
    ).astype(jnp.bfloat16).reshape(tokens, msa_rows * value_width)
    places = lax.dynamic_index_in_dim(jnp.asarray(places), col_index, 0, keepdims=False)
    sequence_slab = sequence_embedding.reshape(msa_rows, columns_here, features).astype(jnp.float32)
    sequence_normed = apply_layer_norm(sequence_slab, 2).astype(jnp.bfloat16)
    sequence_switch = jax.nn.sigmoid(
        jnp.einsum(
            "sjf,fg->jsg",
            sequence_normed,
            sequence_entry_matrix[:, value_width:],
            preferred_element_type=jnp.float32,
        )
    ).reshape(columns_here, msa_rows * value_width)
    blank = jnp.zeros_like(sequence_exit_matrix)
    exits = jnp.stack(
        [
            jnp.concatenate([sequence_exit_matrix, blank], axis=1),
            jnp.concatenate([blank, sequence_exit_matrix], axis=1),
        ]
    )
    mine, values, sequence_switch, exits, places = lax.optimization_barrier(
        (mine, values, sequence_switch, exits, places)
    )
    swap = [(a, (a + col_size) % row_size) for a in range(row_size)]
    other = lax.ppermute(mine, "row", swap)

    half_index = row_index // col_size

    mine_places = lax.dynamic_index_in_dim(places, half_index, 0, keepdims=False)
    other_places = lax.dynamic_index_in_dim(places, 1 - half_index, 0, keepdims=False)
    across = msa_rows * value_width
    averaging = [
        pltpu.VMEM(mine.shape, jnp.float32),
        pltpu.VMEM((tokens, rows_here * heads), jnp.float32),
    ]
    flops = 2 * tokens * rows_here * heads * across
    mine = pl.pallas_call(
        functools.partial(average, value_width),
        out_shape=jax.ShapeDtypeStruct((rows_here, across), jnp.float32),
        in_specs=[smem, vmem, vmem],
        out_specs=vmem,
        scratch_shapes=averaging,
        compiler_params=spacious,
        cost_estimate=work(flops),
    )(mine_places, mine, values)
    sequence_refreshed = pl.pallas_call(
        functools.partial(finish_kernel, value_width, features),
        out_shape=jax.ShapeDtypeStruct(sequence_embedding.shape, jnp.bfloat16),
        in_specs=[smem, smem] + [vmem] * 6,
        out_specs=vmem,
        scratch_shapes=[pltpu.VMEM((rows_here, across), jnp.float32)]
        + averaging
        + [
            pltpu.VMEM(tiled(columns_here, across), jnp.float32),
            pltpu.VMEM((msa_rows * rows_here, 2 * features), jnp.float32),
        ],
        compiler_params=spacious,
        cost_estimate=work(flops),
    )(
        other_places,
        sequence_present_flags,
        other,
        values,
        mine,
        sequence_switch,
        exits,
        sequence_embedding,
    )
    return coupling_refreshed, sequence_refreshed


def solution(mesh):
    placed = (P("row", "col", None), P("row", "col"), P(), P("row"), P(), P(), P(), P(), P())
    return jax.shard_map(
        shards,
        mesh=mesh,
        in_specs=placed,
        out_specs=(P("row", "col", None), P("row", "col")),
        check_vma=False,
    )
```
